32 devices in a mesh: dp: 8 (over z, x), mp: 4 (over y, core).
Axes of the slice: x: 2, y: 2, z: 4, core: 2. Of those that a mesh axis runs over, the one named last changes fastest.
Arguments:
- tokens: bfloat16 [8192, 8192], P(('dp', 'mp')), may hold values from -6 to 6
- key_value_weight: bfloat16 [8192, 2048], P(None, 'mp'), may hold values from -0.0625 to 0.0625
- adapter_down_weight: bfloat16 [16, 8192, 128], P(None, ('dp', 'mp')), may hold values from -0.0625 to 0.0625
- adapter_up_weight: bfloat16 [16, 64, 2048], P(None, 'dp', 'mp'), may hold values from -1 to 1
- adapter_per_request: int32 [32], replicated, may hold values from 0 to 15
- request_per_segment: int32 [64], replicated, may hold values from 0 to 31, never falling along the last dimension, each value on 1 to 4 neighbouring positions
Outputs:
- kv_out: bfloat16 [8192, 2048], P('dp', 'mp')
The draws below stay inside these ranges and needn't reach their ends.
Inputs may be any that keep to these rules, and one draw needn't show every extreme that they name: request_per_segment never falls along the segments; every request has 1 to 4 segments, one has exactly 4.
All inputs are finite; a program needn't handle non-finite values.
Results may differ from the reference program's by a relative error of at most 0.0043.
Values may be sent and summed in bfloat16 or wider, within the bound.
A program may use at most 128 MiB of HBM per device.

```python
import math
import jax
import jax.numpy as jnp
import numpy as np
from jax import lax

MODEL_WIDTH = 8192
KEY_VALUE_WIDTH = 1024
ADAPTER_RANK = 64
SEG = 128
ADAPTER_TOTAL = 16
SEGS = 64
REQUESTS = 32
TOKENS = 8192


def plant(array, key, least, high):
    dims = array.shape
    place = [jax.random.randint(jax.random.fold_in(key, axis), (), 0, dims[axis]) for axis in range(len(dims))]
    array = array.at[tuple(place)].set(least)
    longest = dims.index(max(dims))
    place[longest] = (place[longest] + 1) % dims[longest]
    return array.at[tuple(place)].set(high)


def block_levels(own_key, dims, split, low, largest):
    loudness = 1.0
    for position, shards_of in split:
        heights = jax.random.uniform(jax.random.fold_in(jax.random.fold_in(own_key, 6), position), (shards_of,), jnp.float32, low / len(split), largest / len(split))
        loudness = loudness * jnp.repeat(jnp.exp(heights), dims[position] // shards_of).reshape((-1,) + (1,) * (len(dims) - 1 - position))
    return loudness


def rank_bounds(number_of, skew):
    portions = [(1 << 20) // math.isqrt(standing ** skew) + 1 for standing in range(1, number_of + 1)]
    scale = 1 + sum(portions) // (1 << 30)
    return np.cumsum(np.array([max(1, weight // scale) for weight in portions]))


def ranked(stream_key, extent, amount, slope):
    table = rank_bounds(amount, slope)
    lot = jax.random.randint(jax.random.fold_in(stream_key, 1), extent, 0, int(table[amount - 1]))
    standing = jnp.searchsorted(jnp.asarray(table, jnp.int32), lot, side="right")
    return jax.random.permutation(jax.random.fold_in(stream_key, 2), amount)[standing].astype(jnp.int32)


def profile(count, total, reach, slope):
    weights = [(1 << 20) // math.isqrt(standing ** slope) + 1 for standing in range(2, count + 1)]
    surplus, counts = total - reach - (count - 1), [1] * (count - 1)
    while surplus > 0:
        candidates = [i for i in range(count - 1) if counts[i] < reach]
        whole, remaining = sum([weights[i] for i in candidates]), surplus
        for i in candidates:
            addition = min(reach - counts[i], max(1, remaining * weights[i] // whole), surplus)
            counts[i] = counts[i] + addition
            surplus = surplus - addition
    return np.array([reach] + counts)


def uneven(stream_key, number_of, total, bound, slope):
    if number_of == 2:
        one = jax.random.randint(stream_key, (), max(1, total - bound), min(bound, total - 1) + 1)
        return jnp.stack([one, total - one])
    tallies = jnp.asarray(profile(number_of, total, bound, slope), jnp.int32)
    twos = (number_of - 1) // 2
    donor, sink = tallies[1:1 + 2 * twos:2], tallies[2:2 + 2 * twos:2]
    room = jnp.minimum(donor - 1, bound - sink)
    passed = jax.random.randint(jax.random.fold_in(stream_key, 1), (twos,), 0, 1 << 20) % (room + 1)
    tallies = tallies.at[1:1 + 2 * twos:2].set(donor - passed).at[2:2 + 2 * twos:2].set(sink + passed)
    return tallies[jax.random.permutation(jax.random.fold_in(stream_key, 2), number_of)]


def scatter_about(key, shape, spread, bound, cuts=(), kind=jnp.bfloat16):
    level = block_levels(key, shape, cuts, -0.22, 0.18) if cuts else 1.0
    entries = jax.random.normal(key, shape, jnp.float32) * spread * level
    return jnp.minimum(jnp.maximum(entries, -bound), bound).astype(kind)


def setup_inputs(seed: int = 0) -> dict:
    seeds = jax.random.split(jax.random.key(seed), 7)
    return {
        "tokens": scatter_about(seeds[0], (TOKENS, MODEL_WIDTH), 1.0, 6.0, ((0, 32),)),
        "key_value_weight": scatter_about(seeds[1], (MODEL_WIDTH, 2 * KEY_VALUE_WIDTH), MODEL_WIDTH ** -0.5, 0.0625, ((1, 4),)),
        "adapter_down_weight": scatter_about(seeds[2], (ADAPTER_TOTAL, MODEL_WIDTH, 2 * ADAPTER_RANK), MODEL_WIDTH ** -0.5, 0.0625, ((1, 32),)),
        "adapter_up_weight": scatter_about(seeds[3], (ADAPTER_TOTAL, ADAPTER_RANK, 2 * KEY_VALUE_WIDTH), (ADAPTER_RANK // 2) ** -0.5, 1.0, ((1, 8), (2, 4))),
        "adapter_per_request": plant(ranked(seeds[4], (REQUESTS,), ADAPTER_TOTAL, 2), jax.random.fold_in(seeds[4], 3), 0, ADAPTER_TOTAL - 1).astype(jnp.int32),
        "request_per_segment": jnp.searchsorted(jnp.cumsum(uneven(seeds[5], REQUESTS, SEGS, 4, 2)), jnp.arange(SEGS), side="right").astype(jnp.int32),
    }


def reference(tokens, key_value_weight, adapter_down_weight, adapter_up_weight, adapter_per_request, request_per_segment):
    seg_adapter = jnp.take(adapter_per_request, request_per_segment, axis=0).astype(jnp.int32)
    base = jnp.dot(tokens, key_value_weight, preferred_element_type=jnp.float32)
    count = request_per_segment.shape[0]
    partial_outputs = tokens.reshape(count, SEG, MODEL_WIDTH)

    def one_segment(position_index):
        adapter_choice = seg_adapter[position_index]
        rank_output = jnp.dot(partial_outputs[position_index], adapter_down_weight[adapter_choice], preferred_element_type=jnp.float32).astype(jnp.bfloat16)
        selected_up_weight = adapter_up_weight[adapter_choice]
        key_part = jnp.dot(rank_output[:, :ADAPTER_RANK], selected_up_weight[:, :KEY_VALUE_WIDTH], preferred_element_type=jnp.float32)
        value_part = jnp.dot(rank_output[:, ADAPTER_RANK:], selected_up_weight[:, KEY_VALUE_WIDTH:], preferred_element_type=jnp.float32)
        return jnp.concatenate([key_part, value_part], axis=1)

    delta = lax.map(one_segment, jnp.arange(count, dtype=jnp.int32))
    return (base + delta.reshape(count * SEG, 2 * KEY_VALUE_WIDTH)).astype(jnp.bfloat16)
```

```python
import functools

import jax
import jax.numpy as jnp
import numpy as np
from jax import lax
from jax.experimental import pallas as pl
from jax.experimental.pallas import tpu as pltpu
from jax.sharding import PartitionSpec as P

MESH = pl.DeviceIdType.MESH
AHEAD = 6


def plain(
    tokens,
    key_value_weight,
    adapter_down_weight,
    adapter_up_weight,
    adapter_per_request,
    request_per_segment,
):
    n_dp = lax.axis_size("dp")
    n_mp = lax.axis_size("mp")
    group = lax.axis_index("dp")
    column = lax.axis_index("mp")
    seg_total = request_per_segment.shape[0]
    seg_group = seg_total // n_dp
    seg_adapter = jnp.take(adapter_per_request, request_per_segment, axis=0)
    local_portion = lax.dynamic_slice_in_dim(seg_adapter, group * seg_group, seg_group)
    gathered = lax.all_gather(tokens, "mp", axis=0, tiled=True)
    rows = gathered.shape[0]
    seg_len = rows // seg_group
    width_tile = adapter_down_weight.shape[1]
    double_rank = adapter_down_weight.shape[2]
    rank = double_rank // 2
    column_tile = adapter_up_weight.shape[2]
    base = jnp.dot(gathered, key_value_weight, preferred_element_type=jnp.float32)
    strided = lax.dynamic_index_in_dim(
        gathered.reshape(rows, n_dp, n_mp, width_tile), column, 2, keepdims=False
    ).reshape(seg_group, seg_len, n_dp * width_tile)
    selected_factor = jnp.take(
        lax.all_gather(adapter_down_weight, "dp", axis=1, tiled=True), local_portion, axis=0
    )
    partial_low = jnp.einsum(
        "sti,sir->str", strided, selected_factor, preferred_element_type=jnp.float32
    )
    selected_factor = jnp.take(
        lax.all_gather(adapter_up_weight, "dp", axis=1, tiled=True), local_portion, axis=0
    )
    rank_output = lax.psum(partial_low, "mp").astype(jnp.bfloat16)
    key_width = n_mp * column_tile // 2
    half = column * column_tile // key_width
    low_half = lax.dynamic_slice_in_dim(rank_output, half * rank, rank, 2)
    delta = jnp.einsum(
        "str,src->stc", low_half, selected_factor, preferred_element_type=jnp.float32
    )
    return (base + delta.reshape(rows, column_tile)).astype(jnp.bfloat16)


def kernel(
    n_dp,
    sel,
    target,
    owner_adapter,
    tok,
    weight,
    down,
    up,
    out,
    t_all,
    w_all,
    d_all,
    u_all,
    acc,
    part,
    part_in,
    swap_out,
    swap_in,
    low,
    u_sel,
    local_sem,
    pair_send,
    pair_recv,
    y_send,
    y_recv,
    fwd_send,
    fwd_recv,
    d_send,
    d_recv,
    u_send,
    u_recv,
    hop_send,
    hop_recv,
):
    group = lax.axis_index("dp")
    me = lax.axis_index("mp")
    y, core = me // 2, me % 2
    other_y = 1 - y
    sibling = y * 2 + (1 - core)
    across = other_y * 2 + core
    diagonal = other_y * 2 + (1 - core)

    rows, depth = tok.shape
    adapters, tile, double_rank = down.shape
    rank = double_rank // 2
    up_rows = up.shape[0]
    pieces = 2 * n_dp
    piece = 2 * tile
    last = n_dp - 1
    span = n_dp // 2
    half_tile = tile // 2
    half_adapters = adapters // 2

    z, x = group // 2, group % 2
    place = z + x * (n_dp - 1 - 2 * z)

    def at_place(q):
        q = (q + 2 * n_dp) % n_dp
        side, step = q // span, q % span
        return (step + side * (span - 1 - 2 * step)) * 2 + side

    after, before = at_place(place + 1), at_place(place - 1)

    barrier = pltpu.get_barrier_semaphore()
    for partner in ((after, me), (before, me), (group, across), (group, sibling)):
        pl.semaphore_signal(barrier, inc=1, device_id=partner, device_id_type=MESH)
    pl.semaphore_wait(barrier, 4)

    def remote(src, dst, send, recv, partner):
        return pltpu.make_async_remote_copy(
            src_ref=src, dst_ref=dst, send_sem=send, recv_sem=recv,
            device_id=partner, device_id_type=MESH,
        )

    def d_part(ref, way, sub):
        return ref.at[
            pl.ds(sub * half_adapters, half_adapters), pl.ds(way * half_tile, half_tile)
        ]

    def sent_block(way, step):
        return at_place(place - step) if way == 0 else at_place(place + step)

    def d_copy(way, step, sub, block, src):
        return remote(
            d_part(src, way, sub), d_part(d_all.at[block], way, sub),
            d_send.at[way, step, sub], d_recv.at[way, step, sub],
            (after if way == 0 else before, me),
        )

    def u_copy(way, step, block, src, first):
        half = up_rows // 2
        there = pl.ds(pl.multiple_of(block * up_rows + way * half, half), half)
        here = pl.ds(way * half, half) if first else there
        return remote(
            src.at[here], u_all.at[there],
            u_send.at[way, step], u_recv.at[way, step],
            (after if way == 0 else before, me),
        )

    def columns(i, side):
        start = (i % n_dp) * (4 * tile) + ((side + i // n_dp) % 2) * piece
        return pl.ds(pl.multiple_of(start, piece), piece)

    def y_copy(i):
        cols = columns(i, other_y)
        return remote(
            tok.at[:, cols], t_all.at[me, :, cols], y_send.at[i], y_recv.at[i], (group, across)
        )

    def y_arrival(i):
        cols = columns(i, y)
        return remote(
            tok.at[:, cols], t_all.at[across, :, cols], y_send.at[i], y_recv.at[i],
            (group, across),
        )

    def fwd_copy(i):
        cols = columns(i, y)
        return remote(
            t_all.at[across, :, cols], t_all.at[across, :, cols],
            fwd_send.at[i], fwd_recv.at[i], (group, sibling),
        )

    def fwd_arrival(i):
        cols = columns(i, y)
        return remote(
            t_all.at[diagonal, :, cols], t_all.at[diagonal, :, cols],
            fwd_send.at[i], fwd_recv.at[i], (group, sibling),
        )

    for sub in range(2):
        for way in range(2):
            d_copy(way, 0, sub, group, down).start()
    for way in range(2):
        u_copy(way, 0, group, up, True).start()
    for i in range(AHEAD):
        y_copy(i).start()
    t_local = pltpu.make_async_copy(tok, t_all.at[me], local_sem.at[0])
    w_local = pltpu.make_async_copy(weight, w_all, local_sem.at[1])
    d_local = pltpu.make_async_copy(down, d_all.at[group], local_sem.at[2])
    u_local = pltpu.make_async_copy(
        up, u_all.at[pl.ds(pl.multiple_of(group * up_rows, up_rows), up_rows)], local_sem.at[3]
    )
    t_local.start()
    w_local.start()
    d_local.start()
    u_local.start()
    pair = remote(tok, t_all.at[me], pair_send, pair_recv, (group, sibling))
    pair.start()

    acc[...] = jnp.zeros_like(acc)

    def add(block, cols):
        acc[block] += jnp.dot(
            t_all[block, :, cols], w_all[cols, :], preferred_element_type=jnp.float32
        )

    def add_whole(block):
        @pl.loop(0, n_dp)
        def _(k):
            add(block, pl.ds(pl.multiple_of(k * 4 * tile, 4 * tile), 4 * tile))

    t_local.wait()
    w_local.wait()
    add_whole(me)

    def take_piece(i):
        y_arrival(i).wait_recv()
        fwd_copy(i).start()
        y_copy(i).wait_send()

        @pl.when(i + AHEAD < pieces)
        def _():
            y_copy(i + AHEAD).start()

        add(across, columns(i, y))

        @pl.when(i > 0)
        def _():
            fwd_arrival(i - 1).wait_recv()
            add(diagonal, columns(i - 1, y))

    @pl.loop(0, last)
    def _(step):
        for sub in range(2):
            for way in range(2):
                block = at_place(place - 1 - step) if way == 0 else at_place(place + 1 + step)
                d_copy(way, step, sub, block, d_all.at[block]).wait_recv()

                @pl.when(step + 1 < last)
                def _():
                    d_copy(way, step + 1, sub, block, d_all.at[block]).start()
        for way in range(2):
            block = at_place(place - 1 - step) if way == 0 else at_place(place + 1 + step)
            u_copy(way, step, block, u_all, False).wait_recv()

            @pl.when(step + 1 < last)
            def _():
                u_copy(way, step + 1, block, u_all, False).start()

        @pl.when(step == 0)
        def _():
            remote(tok, t_all.at[sibling], pair_send, pair_recv, (group, sibling)).wait_recv()
            add_whole(sibling)

        @pl.when(step > 0)
        def _():
            @pl.loop(2 * step - 2, 2 * step)
            def _(i):
                take_piece(i)

    d_local.wait()
    u_local.wait()

    segs = sel.shape[0]
    seg_block = segs // 4
    seg_len = rows // seg_block

    def partial_low(c):
        @pl.loop(0, 2 * seg_block)
        def _(k):
            yy, inner = k // seg_block, k % seg_block
            block = yy * 2 + c
            adapter = sel[block * seg_block + inner]
            span_rows = pl.ds(pl.multiple_of(inner * seg_len, seg_len), seg_len)
            total = jnp.zeros((seg_len, double_rank), jnp.float32)
            for g in range(n_dp):
                cols = pl.ds(pl.multiple_of(g * 4 * tile + me * tile, tile), tile)
                total += jnp.dot(
                    t_all[block, span_rows, cols], d_all[g, adapter],
                    preferred_element_type=jnp.float32,
                )
            part[c, yy, span_rows, :] = total

    partial_low(1 - core)
    hop1 = remote(part.at[1 - core], part_in, hop_send.at[0], hop_recv.at[0], (group, sibling))
    hop1.start()
    partial_low(core)
    hop1.wait_recv()
    q0 = part[core, 0] + part_in[0]
    q1 = part[core, 1] + part_in[1]
    key_part = jnp.concatenate([q0[:, :rank], q1[:, :rank]], axis=1)
    value_part = jnp.concatenate([q0[:, rank:], q1[:, rank:]], axis=1)
    swap_out[0] = jnp.where(y == 0, value_part, key_part)
    swap_out[1] = jnp.where(y == 0, key_part, value_part)
    hop2 = remote(swap_out.at[0], swap_in, hop_send.at[1], hop_recv.at[1], (group, across))
    hop2.start()

    @pl.loop(0, segs)
    def _(s):
        yy = s // (2 * seg_block)
        line = lax.broadcasted_iota(jnp.int32, (double_rank, u_all.shape[0]), 0)
        hit = (line == target[...] + yy * rank) & (owner_adapter[...] == sel[s])
        pick = jnp.where(hit, 1.0, 0.0).astype(jnp.bfloat16)
        u_sel[s] = jnp.dot(pick, u_all[...], preferred_element_type=jnp.float32).astype(
            jnp.bfloat16
        )

    @pl.loop(2 * (last - 1), pieces)
    def _(i):
        take_piece(i)

    hop2.wait_recv()
    low[core] = (swap_out[1] + swap_in[...]).astype(jnp.bfloat16)
    hop3 = remote(low.at[core], low.at[core], hop_send.at[2], hop_recv.at[2], (group, sibling))
    hop3.start()
    fwd_arrival(pieces - 1).wait_recv()
    add(diagonal, columns(pieces - 1, y))

    def finish(c):
        @pl.loop(0, 2 * seg_block)
        def _(k):
            yy, inner = k // seg_block, k % seg_block
            block = yy * 2 + c
            span_rows = pl.ds(pl.multiple_of(inner * seg_len, seg_len), seg_len)
            delta = jnp.dot(
                low[c, span_rows, :], u_sel[block * seg_block + inner],
                preferred_element_type=jnp.float32,
            )
            out[block, span_rows, :] = (acc[block, span_rows, :] + delta).astype(jnp.bfloat16)

    finish(core)
    remote(
        low.at[1 - core], low.at[1 - core], hop_send.at[2], hop_recv.at[2], (group, sibling)
    ).wait_recv()
    finish(1 - core)

    pair.wait_send()
    hop1.wait_send()
    hop2.wait_send()
    hop3.wait_send()

    @pl.loop(0, pieces)
    def _(i):
        fwd_copy(i).wait_send()

    @pl.loop(0, last)
    def _(step):
        for way in range(2):
            block = sent_block(way, step)
            for sub in range(2):
                d_copy(way, step, sub, block, d_all.at[block]).wait_send()
            u_copy(way, step, block, u_all, False).wait_send()


def on_device(
    tokens,
    key_value_weight,
    adapter_down_weight,
    adapter_up_weight,
    adapter_per_request,
    request_per_segment,
):
    n_dp = lax.axis_size("dp")
    n_mp = lax.axis_size("mp")
    rows, depth = tokens.shape
    width = key_value_weight.shape[1]
    adapters, tile, double_rank = adapter_down_weight.shape
    up_rank = adapter_up_weight.shape[1]
    if n_mp != 4 or tile % 256 or (adapters * up_rank) % 32 or n_dp % 2:
        return plain(
            tokens, key_value_weight, adapter_down_weight, adapter_up_weight,
            adapter_per_request, request_per_segment,
        )
    seg_group = request_per_segment.shape[0] // n_dp
    mine = lax.dynamic_slice_in_dim(
        request_per_segment, lax.axis_index("dp") * seg_group, seg_group
    )
    sel = jnp.take(adapter_per_request, mine, axis=0)
    up_rows = adapters * up_rank
    index = np.arange(n_dp * up_rows)
    target = jnp.asarray((index // up_rows * up_rank + index % up_rank)[None], jnp.int32)
    owner_adapter = jnp.asarray((index // up_rank % adapters)[None], jnp.int32)
    last = n_dp - 1
    bf16, f32 = jnp.bfloat16, jnp.float32
    dma = pltpu.SemaphoreType.DMA
    vmem = pl.BlockSpec(memory_space=pltpu.VMEM)
    result = pl.pallas_call(
        functools.partial(kernel, n_dp),
        out_shape=jax.ShapeDtypeStruct((n_mp, rows, width), bf16),
        in_specs=[pl.BlockSpec(memory_space=pltpu.SMEM), vmem, vmem]
        + [pl.BlockSpec(memory_space=pl.ANY)] * 4,
        out_specs=vmem,
        scratch_shapes=[
            pltpu.VMEM((n_mp, rows, depth), bf16),
            pltpu.VMEM((depth, width), bf16),
            pltpu.VMEM((n_dp, adapters, tile, double_rank), bf16),
            pltpu.VMEM((n_dp * up_rows, width), bf16),
            pltpu.VMEM((n_mp, rows, width), f32),
            pltpu.VMEM((2, 2, rows, double_rank), f32),
            pltpu.VMEM((2, rows, double_rank), f32),
            pltpu.VMEM((2, rows, double_rank), f32),
            pltpu.VMEM((rows, double_rank), f32),
            pltpu.VMEM((2, rows, double_rank), bf16),
            pltpu.VMEM((seg_group, double_rank, width), bf16),
            dma((4,)),
            dma,
            dma,
            dma((2 * n_dp,)),
            dma((2 * n_dp,)),
            dma((2 * n_dp,)),
            dma((2 * n_dp,)),
            dma((2, last, 2)),
            dma((2, last, 2)),
            dma((2, last)),
            dma((2, last)),
            dma((3,)),
            dma((3,)),
        ],
        compiler_params=pltpu.CompilerParams(
            collective_id=0, has_side_effects=True, vmem_limit_bytes=52 * 2**20
        ),
    )(
        sel, target, owner_adapter, tokens, key_value_weight, adapter_down_weight,
        adapter_up_weight.reshape(up_rows, width),
    )
    return result.reshape(n_mp * rows, width)


def solution(mesh):
    placed = (
        P(("dp", "mp"), None),
        P(None, "mp"),
        P(None, ("dp", "mp"), None),
        P(None, "dp", "mp"),
        P(),
        P(),
    )
    return jax.shard_map(
        on_device, mesh=mesh, in_specs=placed, out_specs=P("dp", "mp"), check_vma=False
    )
```

```python
import functools

import jax
import jax.numpy as jnp
from jax import lax
from jax.experimental import pallas as pl
from jax.experimental.pallas import tpu as pltpu
from jax.sharding import PartitionSpec as P

MESH = pl.DeviceIdType.MESH
AHEAD = 4


def plain(
    tokens,
    key_value_weight,
    adapter_down_weight,
    adapter_up_weight,
    adapter_per_request,
    request_per_segment,
):
    n_dp = lax.axis_size("dp")
    n_mp = lax.axis_size("mp")
    group = lax.axis_index("dp")
    column = lax.axis_index("mp")
    seg_total = request_per_segment.shape[0]
    seg_group = seg_total // n_dp
    seg_adapter = jnp.take(adapter_per_request, request_per_segment, axis=0)
    local_portion = lax.dynamic_slice_in_dim(seg_adapter, group * seg_group, seg_group)
    gathered = lax.all_gather(tokens, "mp", axis=0, tiled=True)
    rows = gathered.shape[0]
    seg_len = rows // seg_group
    width_tile = adapter_down_weight.shape[1]
    double_rank = adapter_down_weight.shape[2]
    rank = double_rank // 2
    column_tile = adapter_up_weight.shape[2]
    base = jnp.dot(gathered, key_value_weight, preferred_element_type=jnp.float32)
    strided = lax.dynamic_index_in_dim(
        gathered.reshape(rows, n_dp, n_mp, width_tile), column, 2, keepdims=False
    ).reshape(seg_group, seg_len, n_dp * width_tile)
    selected_factor = jnp.take(
        lax.all_gather(adapter_down_weight, "dp", axis=1, tiled=True), local_portion, axis=0
    )
    partial_low = jnp.einsum(
        "sti,sir->str", strided, selected_factor, preferred_element_type=jnp.float32
    )
    selected_factor = jnp.take(
        lax.all_gather(adapter_up_weight, "dp", axis=1, tiled=True), local_portion, axis=0
    )
    rank_output = lax.psum(partial_low, "mp").astype(jnp.bfloat16)
    key_width = n_mp * column_tile // 2
    half = column * column_tile // key_width
    low_half = lax.dynamic_slice_in_dim(rank_output, half * rank, rank, 2)
    delta = jnp.einsum(
        "str,src->stc", low_half, selected_factor, preferred_element_type=jnp.float32
    )
    return (base + delta.reshape(rows, column_tile)).astype(jnp.bfloat16)


def kernel(
    n_dp,
    up_rank,
    requests,
    segments,
    tok,
    weight,
    down,
    up,
    out,
    t_all,
    w_all,
    d_own,
    d_one,
    d_two,
    d_three,
    d_three_picked,
    d_four_picked,
    stage_three,
    stage_four,
    u_all,
    acc,
    part,
    part_in,
    swap_out,
    swap_in,
    low,
    u_sel,
    local_sem,
    pair_send,
    pair_recv,
    y_send,
    y_recv,
    fwd_send,
    fwd_recv,
    d_send,
    d_recv,
    u_send,
    u_recv,
    hop_send,
    hop_recv,
):
    group = lax.axis_index("dp")
    me = lax.axis_index("mp")
    y, core = me // 2, me % 2
    other_y = 1 - y
    sibling = y * 2 + (1 - core)
    across = other_y * 2 + core
    diagonal = other_y * 2 + (1 - core)

    rows, depth = tok.shape
    adapters, tile, double_rank = down.shape
    rank = double_rank // 2
    up_rows = up.shape[0]
    pieces = 2 * n_dp
    piece = 2 * tile
    span = n_dp // 2
    half_tile = tile // 2
    quarter = adapters // 4
    segs = segments.shape[0] // n_dp
    seg_block = segs // 4
    seg_len = rows // seg_block

    z, x = group // 2, group % 2
    place = z + x * (n_dp - 1 - 2 * z)

    def at_place(q):
        q = (q + 2 * n_dp) % n_dp
        side, step = q // span, q % span
        return (step + side * (span - 1 - 2 * step)) * 2 + side

    after, before = at_place(place + 1), at_place(place - 1)
    onward = (after, before)

    def adapter_of(g, seg):
        return requests[segments[g * segs + seg]]

    barrier = pltpu.get_barrier_semaphore()
    for partner in ((after, me), (before, me), (group, across), (group, sibling)):
        pl.semaphore_signal(barrier, inc=1, device_id=partner, device_id_type=MESH)
    pl.semaphore_wait(barrier, 4)

    def remote(src, dst, send, recv, partner):
        return pltpu.make_async_remote_copy(
            src_ref=src, dst_ref=dst, send_sem=send, recv_sem=recv,
            device_id=partner, device_id_type=MESH,
        )

    def quarter_of(k):
        return pl.ds(k * quarter, quarter)

    def one(way, k):
        return remote(
            down.at[quarter_of(k)], d_one.at[way, quarter_of(k)],
            d_send.at[way, k], d_recv.at[way, k], (onward[way], me),
        )

    def two(way, k):
        return remote(
            d_one.at[way, quarter_of(k)], d_two.at[way, quarter_of(k)],
            d_send.at[way, 4 + k], d_recv.at[way, 4 + k], (onward[way], me),
        )

    def three(way, k):
        return remote(
            d_two.at[way, quarter_of(k), pl.ds(way * half_tile, half_tile)],
            d_three.at[way, quarter_of(k)],
            d_send.at[way, 8 + k], d_recv.at[way, 8 + k], (onward[way], me),
        )

    def three_picked(way):
        return remote(
            stage_three.at[way], d_three_picked.at[way],
            d_send.at[way, 12], d_recv.at[way, 12], (onward[way], me),
        )

    def four_picked(way):
        return remote(
            stage_four.at[way], d_four_picked.at[way],
            d_send.at[way, 13], d_recv.at[way, 13], (onward[way], me),
        )

    def u_rows(way, step, block):
        if step < span - 1:
            return pl.ds(pl.multiple_of(block * up_rows, up_rows), up_rows)
        half = up_rows // 2
        return pl.ds(pl.multiple_of(block * up_rows + way * half, half), half)

    def u_copy(way, step):
        block = at_place(place - step) if way == 0 else at_place(place + step)
        there = u_rows(way, step, block)
        return remote(
            up if step == 0 else u_all.at[there], u_all.at[there],
            u_send.at[way, step], u_recv.at[way, step], (onward[way], me),
        )

    def u_arrival(way, step):
        block = at_place(place - 1 - step) if way == 0 else at_place(place + 1 + step)
        there = u_rows(way, step, block)
        return remote(
            u_all.at[there], u_all.at[there],
            u_send.at[way, step], u_recv.at[way, step], (onward[way], me),
        )

    def near(k):
        return at_place(place + (k + 1) // 2 * (1 - 2 * (k % 2)))

    def columns(i, side):
        start = near(i % n_dp) * (4 * tile) + ((side + i // n_dp) % 2) * piece
        return pl.ds(pl.multiple_of(start, piece), piece)

    def y_copy(i):
        cols = columns(i, other_y)
        return remote(
            tok.at[:, cols], t_all.at[me, :, cols], y_send.at[i], y_recv.at[i], (group, across)
        )

    def y_arrival(i):
        cols = columns(i, y)
        return remote(
            tok.at[:, cols], t_all.at[across, :, cols], y_send.at[i], y_recv.at[i],
            (group, across),
        )

    def fwd_copy(i):
        cols = columns(i, y)
        return remote(
            t_all.at[across, :, cols], t_all.at[across, :, cols],
            fwd_send.at[i], fwd_recv.at[i], (group, sibling),
        )

    def fwd_arrival(i):
        cols = columns(i, y)
        return remote(
            t_all.at[diagonal, :, cols], t_all.at[diagonal, :, cols],
            fwd_send.at[i], fwd_recv.at[i], (group, sibling),
        )

    for i in range(AHEAD):
        y_copy(i).start()
    for k in range(4):
        for way in range(2):
            one(way, k).start()
    for way in range(2):
        u_copy(way, 0).start()
    t_local = pltpu.make_async_copy(tok, t_all.at[me], local_sem.at[0])
    w_local = pltpu.make_async_copy(weight, w_all, local_sem.at[1])
    d_local = pltpu.make_async_copy(down, d_own, local_sem.at[2])
    u_local = pltpu.make_async_copy(
        up, u_all.at[pl.ds(pl.multiple_of(group * up_rows, up_rows), up_rows)], local_sem.at[3]
    )
    t_local.start()
    w_local.start()
    d_local.start()
    u_local.start()
    pair = remote(tok, t_all.at[me], pair_send, pair_recv, (group, sibling))
    pair.start()

    acc[...] = jnp.zeros_like(acc)
    part[...] = jnp.zeros_like(part)

    def add(block, cols):
        acc[block] += jnp.dot(
            t_all[block, :, cols], w_all[cols, :], preferred_element_type=jnp.float32
        )

    def add_whole(block):
        @pl.loop(0, n_dp)
        def _(k):
            add(block, pl.ds(pl.multiple_of(k * 4 * tile, 4 * tile), 4 * tile))

    def take_piece(i):
        y_arrival(i).wait_recv()
        fwd_copy(i).start()
        y_copy(i).wait_send()

        @pl.when(i + AHEAD < pieces)
        def _():
            y_copy(i + AHEAD).start()

        add(across, columns(i, y))

        @pl.when(i > 0)
        def _():
            fwd_arrival(i - 1).wait_recv()
            add(diagonal, columns(i - 1, y))

    def add_low(blocks, factors):
        @pl.loop(0, segs)
        def _(s):
            block, inner = s // seg_block, s % seg_block
            span_rows = pl.ds(pl.multiple_of(inner * seg_len, seg_len), seg_len)
            adapter = adapter_of(group, s)
            total = part[block % 2, block // 2, span_rows, :]
            for g, factor in zip(blocks, factors):
                cols = pl.ds(pl.multiple_of(g * 4 * tile + me * tile, tile), tile)
                total += jnp.dot(
                    t_all[block, span_rows, cols], factor(adapter, s),
                    preferred_element_type=jnp.float32,
                )
            part[block % 2, block // 2, span_rows, :] = total

    t_local.wait()
    w_local.wait()
    add_whole(me)

    @pl.loop(0, 4)
    def _(k):
        for way in range(2):
            one(way, k).wait_recv()
            two(way, k).start()

        @pl.when(k == 1)
        def _():
            remote(tok, t_all.at[sibling], pair_send, pair_recv, (group, sibling)).wait_recv()
            add_whole(sibling)

        @pl.when(k > 0)
        def _():
            take_piece(k - 1)

    for way in range(2):
        u_arrival(way, 0).wait_recv()
        u_copy(way, 1).start()
    d_local.wait()
    u_local.wait()

    @pl.loop(0, 4)
    def _(k):
        for way in range(2):
            two(way, k).wait_recv()
            three(way, k).start()
        take_piece(k + 3)

        @pl.when(k == 1)
        def _():
            add_low(
                [group, before, after],
                [lambda a, s: d_own[a], lambda a, s: d_one[0, a], lambda a, s: d_one[1, a]],
            )

    @pl.loop(0, segs)
    def _(s):
        for way in range(2):
            stage_three[way, s] = d_two[
                way, adapter_of(onward[way], s), pl.ds((1 - way) * half_tile, half_tile), :
            ]

    for way in range(2):
        three_picked(way).start()
    for way in range(2):
        u_arrival(way, 1).wait_recv()
        u_copy(way, 2).start()
    add_low(
        [at_place(place - 2), at_place(place + 2)],
        [lambda a, s: d_two[0, a], lambda a, s: d_two[1, a]],
    )

    @pl.loop(0, 2)
    def _(h):
        take_piece(h + 7)
        for j in range(2):
            for way in range(2):
                three(way, 2 * h + j).wait_recv()

    @pl.loop(0, segs)
    def _(s):
        for way in range(2):
            stage_four[way, s] = d_three[way, adapter_of(onward[way], s)]

    for way in range(2):
        four_picked(way).start()
    for way in range(2):
        u_arrival(way, 2).wait_recv()
        u_copy(way, 3).start()
    take_piece(9)
    for way in range(2):
        three_picked(way).wait_recv()
    add_low(
        [at_place(place - 3), at_place(place + 3)],
        [
            lambda a, s: jnp.concatenate([d_three[0, a], d_three_picked[0, s]], axis=0),
            lambda a, s: jnp.concatenate([d_three_picked[1, s], d_three[1, a]], axis=0),
        ],
    )
    take_piece(10)
    for way in range(2):
        four_picked(way).wait_recv()
    add_low(
        [at_place(place + 4)],
        [lambda a, s: jnp.concatenate([d_four_picked[0, s], d_four_picked[1, s]], axis=0)],
    )

    hop1 = remote(part.at[1 - core], part_in, hop_send.at[0], hop_recv.at[0], (group, sibling))
    hop1.start()
    hop1.wait_recv()
    q0 = part[core, 0] + part_in[0]
    q1 = part[core, 1] + part_in[1]
    key_part = jnp.concatenate([q0[:, :rank], q1[:, :rank]], axis=1)
    value_part = jnp.concatenate([q0[:, rank:], q1[:, rank:]], axis=1)
    swap_out[0] = jnp.where(y == 0, value_part, key_part)
    swap_out[1] = jnp.where(y == 0, key_part, value_part)
    hop2 = remote(swap_out.at[0], swap_in, hop_send.at[1], hop_recv.at[1], (group, across))
    hop2.start()

    for way in range(2):
        u_arrival(way, 3).wait_recv()

    total_rows = u_all.shape[0]
    index = lax.broadcasted_iota(jnp.int32, (1, total_rows), 1)
    by_group, by_adapter = up_rows.bit_length() - 1, up_rank.bit_length() - 1
    target = lax.shift_right_logical(index, by_group) * up_rank + (index & (up_rank - 1))
    holder = lax.shift_right_logical(index, by_adapter) & (adapters - 1)

    @pl.loop(0, segs)
    def _(s):
        yy = s // (2 * seg_block)
        line = lax.broadcasted_iota(jnp.int32, (double_rank, total_rows), 0)
        hit = (line == target + yy * rank) & (holder == adapter_of(group, s))
        pick = jnp.where(hit, 1.0, 0.0).astype(jnp.bfloat16)
        u_sel[s] = jnp.dot(pick, u_all[...], preferred_element_type=jnp.float32).astype(
            jnp.bfloat16
        )

    @pl.loop(11, pieces - 2)
    def _(i):
        take_piece(i)

    hop2.wait_recv()
    low[core] = (swap_out[1] + swap_in[...]).astype(jnp.bfloat16)
    hop3 = remote(low.at[core], low.at[core], hop_send.at[2], hop_recv.at[2], (group, sibling))
    hop3.start()
    take_piece(pieces - 2)
    remote(
        low.at[1 - core], low.at[1 - core], hop_send.at[2], hop_recv.at[2], (group, sibling)
    ).wait_recv()

    @pl.loop(0, segs)
    def _(s):
        block, inner = s // seg_block, s % seg_block
        span_rows = pl.ds(pl.multiple_of(inner * seg_len, seg_len), seg_len)
        acc[block, span_rows, :] += jnp.dot(
            low[block % 2, span_rows, :], u_sel[s], preferred_element_type=jnp.float32
        )

    out[me] = acc[me].astype(jnp.bfloat16)
    out[sibling] = acc[sibling].astype(jnp.bfloat16)
    take_piece(pieces - 1)
    out[across] = acc[across].astype(jnp.bfloat16)
    fwd_arrival(pieces - 1).wait_recv()
    add(diagonal, columns(pieces - 1, y))
    out[diagonal] = acc[diagonal].astype(jnp.bfloat16)

    pair.wait_send()
    hop1.wait_send()
    hop2.wait_send()
    hop3.wait_send()

    @pl.loop(0, pieces)
    def _(i):
        fwd_copy(i).wait_send()

    for way in range(2):
        for k in range(4):
            one(way, k).wait_send()
            two(way, k).wait_send()
            three(way, k).wait_send()
        three_picked(way).wait_send()
        four_picked(way).wait_send()
        for step in range(4):
            u_copy(way, step).wait_send()


def on_device(
    tokens,
    key_value_weight,
    adapter_down_weight,
    adapter_up_weight,
    adapter_per_request,
    request_per_segment,
):
    n_dp = lax.axis_size("dp")
    n_mp = lax.axis_size("mp")
    rows, depth = tokens.shape
    width = key_value_weight.shape[1]
    adapters, tile, double_rank = adapter_down_weight.shape
    up_rank = adapter_up_weight.shape[1]
    whole_tiles = tile % 256 == 0 and adapters % 4 == 0 and (adapters * up_rank) % 32 == 0
    powers = adapters & (adapters - 1) == 0 and up_rank & (up_rank - 1) == 0
    if n_mp != 4 or n_dp != 8 or not whole_tiles or not powers:
        return plain(
            tokens, key_value_weight, adapter_down_weight, adapter_up_weight,
            adapter_per_request, request_per_segment,
        )
    seg_group = request_per_segment.shape[0] // n_dp
    up_rows = adapters * up_rank
    bf16, f32 = jnp.bfloat16, jnp.float32
    dma = pltpu.SemaphoreType.DMA
    vmem = pl.BlockSpec(memory_space=pltpu.VMEM)
    result = pl.pallas_call(
        functools.partial(kernel, n_dp, up_rank),
        out_shape=jax.ShapeDtypeStruct((n_mp, rows, width), bf16),
        in_specs=[pl.BlockSpec(memory_space=pltpu.SMEM)] * 2
        + [pl.BlockSpec(memory_space=pl.ANY)] * 4,
        out_specs=vmem,
        scratch_shapes=[
            pltpu.VMEM((n_mp, rows, depth), bf16),
            pltpu.VMEM((depth, width), bf16),
            pltpu.VMEM((adapters, tile, double_rank), bf16),
            pltpu.VMEM((2, adapters, tile, double_rank), bf16),
            pltpu.VMEM((2, adapters, tile, double_rank), bf16),
            pltpu.VMEM((2, adapters, tile // 2, double_rank), bf16),
            pltpu.VMEM((2, seg_group, tile // 2, double_rank), bf16),
            pltpu.VMEM((2, seg_group, tile // 2, double_rank), bf16),
            pltpu.VMEM((2, seg_group, tile // 2, double_rank), bf16),
            pltpu.VMEM((2, seg_group, tile // 2, double_rank), bf16),
            pltpu.VMEM((n_dp * up_rows, width), bf16),
            pltpu.VMEM((n_mp, rows, width), f32),
            pltpu.VMEM((2, 2, rows, double_rank), f32),
            pltpu.VMEM((2, rows, double_rank), f32),
            pltpu.VMEM((2, rows, double_rank), f32),
            pltpu.VMEM((rows, double_rank), f32),
            pltpu.VMEM((2, rows, double_rank), bf16),
            pltpu.VMEM((seg_group, double_rank, width), bf16),
            dma((4,)),
            dma,
            dma,
            dma((2 * n_dp,)),
            dma((2 * n_dp,)),
            dma((2 * n_dp,)),
            dma((2 * n_dp,)),
            dma((2, 14)),
            dma((2, 14)),
            dma((2, 4)),
            dma((2, 4)),
            dma((3,)),
            dma((3,)),
        ],
        compiler_params=pltpu.CompilerParams(
            collective_id=0, has_side_effects=True, vmem_limit_bytes=52 * 2**20
        ),
    )(
        adapter_per_request, request_per_segment, tokens, key_value_weight, adapter_down_weight,
        adapter_up_weight.reshape(up_rows, width),
    )
    return result.reshape(n_mp * rows, width)


def solution(mesh):
    placed = (
        P(("dp", "mp"), None),
        P(None, "mp"),
        P(None, ("dp", "mp"), None),
        P(None, "dp", "mp"),
        P(),
        P(),
    )
    return jax.shard_map(
        on_device, mesh=mesh, in_specs=placed, out_specs=P("dp", "mp"), check_vma=False
    )
```

```python
import functools

import jax
import jax.numpy as jnp
from jax import lax
from jax.experimental import pallas as pl
from jax.experimental.pallas import tpu as pltpu
from jax.sharding import PartitionSpec as P

MESH = pl.DeviceIdType.MESH
AHEAD = 6


def plain(
    tokens,
    key_value_weight,
    adapter_down_weight,
    adapter_up_weight,
    adapter_per_request,
    request_per_segment,
):
    n_dp = lax.axis_size("dp")
    n_mp = lax.axis_size("mp")
    group = lax.axis_index("dp")
    column = lax.axis_index("mp")
    seg_total = request_per_segment.shape[0]
    seg_group = seg_total // n_dp
    seg_adapter = jnp.take(adapter_per_request, request_per_segment, axis=0)
    local_portion = lax.dynamic_slice_in_dim(seg_adapter, group * seg_group, seg_group)
    gathered = lax.all_gather(tokens, "mp", axis=0, tiled=True)
    rows = gathered.shape[0]
    seg_len = rows // seg_group
    width_tile = adapter_down_weight.shape[1]
    double_rank = adapter_down_weight.shape[2]
    rank = double_rank // 2
    column_tile = adapter_up_weight.shape[2]
    base = jnp.dot(gathered, key_value_weight, preferred_element_type=jnp.float32)
    strided = lax.dynamic_index_in_dim(
        gathered.reshape(rows, n_dp, n_mp, width_tile), column, 2, keepdims=False
    ).reshape(seg_group, seg_len, n_dp * width_tile)
    selected_factor = jnp.take(
        lax.all_gather(adapter_down_weight, "dp", axis=1, tiled=True), local_portion, axis=0
    )
    partial_low = jnp.einsum(
        "sti,sir->str", strided, selected_factor, preferred_element_type=jnp.float32
    )
    selected_factor = jnp.take(
        lax.all_gather(adapter_up_weight, "dp", axis=1, tiled=True), local_portion, axis=0
    )
    rank_output = lax.psum(partial_low, "mp").astype(jnp.bfloat16)
    key_width = n_mp * column_tile // 2
    half = column * column_tile // key_width
    low_half = lax.dynamic_slice_in_dim(rank_output, half * rank, rank, 2)
    delta = jnp.einsum(
        "str,src->stc", low_half, selected_factor, preferred_element_type=jnp.float32
    )
    return (base + delta.reshape(rows, column_tile)).astype(jnp.bfloat16)


def kernel(
    n_dp,
    up_rank,
    requests,
    segments,
    tok,
    weight,
    down,
    up,
    out,
    t_all,
    w_all,
    d_own,
    d_one,
    d_two,
    d_three,
    d_three_picked,
    d_four_picked,
    stage_three,
    stage_four,
    u_all,
    acc,
    part,
    part_in,
    swap_out,
    swap_in,
    low,
    u_sel,
    local_sem,
    pair_send,
    pair_recv,
    y_send,
    y_recv,
    fwd_send,
    fwd_recv,
    d_send,
    d_recv,
    u_send,
    u_recv,
    hop_send,
    hop_recv,
):
    group = lax.axis_index("dp")
    me = lax.axis_index("mp")
    y, core = me // 2, me % 2
    other_y = 1 - y
    sibling = y * 2 + (1 - core)
    across = other_y * 2 + core
    diagonal = other_y * 2 + (1 - core)

    rows, depth = tok.shape
    adapters, tile, double_rank = down.shape
    rank = double_rank // 2
    up_rows = up.shape[0]
    pieces = 2 * n_dp
    piece = 2 * tile
    span = n_dp // 2
    half_tile = tile // 2
    quarter = adapters // 4
    segs = segments.shape[0] // n_dp
    seg_block = segs // 4
    seg_len = rows // seg_block

    z, x = group // 2, group % 2
    place = z + x * (n_dp - 1 - 2 * z)

    def at_place(q):
        q = (q + 2 * n_dp) % n_dp
        side, step = q // span, q % span
        return (step + side * (span - 1 - 2 * step)) * 2 + side

    after, before = at_place(place + 1), at_place(place - 1)
    onward = (after, before)

    def adapter_of(g, seg):
        return requests[segments[g * segs + seg]]

    barrier = pltpu.get_barrier_semaphore()
    for partner in ((after, me), (before, me), (group, across), (group, sibling)):
        pl.semaphore_signal(barrier, inc=1, device_id=partner, device_id_type=MESH)
    pl.semaphore_wait(barrier, 4)

    def remote(src, dst, send, recv, partner):
        return pltpu.make_async_remote_copy(
            src_ref=src, dst_ref=dst, send_sem=send, recv_sem=recv,
            device_id=partner, device_id_type=MESH,
        )

    def quarter_of(k):
        return pl.ds(k * quarter, quarter)

    def one(way, k):
        return remote(
            down.at[quarter_of(k)], d_one.at[way, quarter_of(k)],
            d_send.at[way, k], d_recv.at[way, k], (onward[way], me),
        )

    def two(way, k):
        return remote(
            d_one.at[way, quarter_of(k)], d_two.at[way, quarter_of(k)],
            d_send.at[way, 4 + k], d_recv.at[way, 4 + k], (onward[way], me),
        )

    def three(way, k):
        return remote(
            d_two.at[way, quarter_of(k), pl.ds(way * half_tile, half_tile)],
            d_three.at[way, quarter_of(k)],
            d_send.at[way, 8 + k], d_recv.at[way, 8 + k], (onward[way], me),
        )

    def three_picked(way):
        return remote(
            stage_three.at[way], d_three_picked.at[way],
            d_send.at[way, 12], d_recv.at[way, 12], (onward[way], me),
        )

    def four_picked(way):
        return remote(
            stage_four.at[way], d_four_picked.at[way],
            d_send.at[way, 13], d_recv.at[way, 13], (onward[way], me),
        )

    def u_rows(way, step, block):
        if step < span - 1:
            return pl.ds(pl.multiple_of(block * up_rows, up_rows), up_rows)
        half = up_rows // 2
        return pl.ds(pl.multiple_of(block * up_rows + way * half, half), half)

    def u_copy(way, step):
        block = at_place(place - step) if way == 0 else at_place(place + step)
        there = u_rows(way, step, block)
        return remote(
            up if step == 0 else u_all.at[there], u_all.at[there],
            u_send.at[way, step], u_recv.at[way, step], (onward[way], me),
        )

    def u_arrival(way, step):
        block = at_place(place - 1 - step) if way == 0 else at_place(place + 1 + step)
        there = u_rows(way, step, block)
        return remote(
            u_all.at[there], u_all.at[there],
            u_send.at[way, step], u_recv.at[way, step], (onward[way], me),
        )

    def near(k):
        return at_place(place + (k + 1) // 2 * (1 - 2 * (k % 2)))

    def columns(i, side):
        start = near(i % n_dp) * (4 * tile) + ((side + i // n_dp) % 2) * piece
        return pl.ds(pl.multiple_of(start, piece), piece)

    def y_copy(i):
        cols = columns(i, other_y)
        return remote(
            tok.at[:, cols], t_all.at[me, :, cols], y_send.at[i], y_recv.at[i], (group, across)
        )

    def y_arrival(i):
        cols = columns(i, y)
        return remote(
            tok.at[:, cols], t_all.at[across, :, cols], y_send.at[i], y_recv.at[i],
            (group, across),
        )

    def fwd_copy(i):
        cols = columns(i, y)
        return remote(
            t_all.at[across, :, cols], t_all.at[across, :, cols],
            fwd_send.at[i], fwd_recv.at[i], (group, sibling),
        )

    def fwd_arrival(i):
        cols = columns(i, y)
        return remote(
            t_all.at[diagonal, :, cols], t_all.at[diagonal, :, cols],
            fwd_send.at[i], fwd_recv.at[i], (group, sibling),
        )

    for i in range(AHEAD):
        y_copy(i).start()
    for k in range(4):
        for way in range(2):
            one(way, k).start()
    t_local = pltpu.make_async_copy(tok, t_all.at[me], local_sem.at[0])
    w_local = pltpu.make_async_copy(weight, w_all, local_sem.at[1])
    d_local = pltpu.make_async_copy(down, d_own, local_sem.at[2])
    u_local = pltpu.make_async_copy(
        up, u_all.at[pl.ds(pl.multiple_of(group * up_rows, up_rows), up_rows)], local_sem.at[3]
    )
    t_local.start()
    w_local.start()
    d_local.start()
    u_local.start()
    pair = remote(tok, t_all.at[me], pair_send, pair_recv, (group, sibling))
    pair.start()

    acc[...] = jnp.zeros_like(acc)
    part[...] = jnp.zeros_like(part)

    def add(block, cols):
        acc[block] += jnp.dot(
            t_all[block, :, cols], w_all[cols, :], preferred_element_type=jnp.float32
        )

    def add_whole(block):
        @pl.loop(0, n_dp)
        def _(k):
            add(block, pl.ds(pl.multiple_of(k * 4 * tile, 4 * tile), 4 * tile))

    def take_piece(i):
        y_arrival(i).wait_recv()
        fwd_copy(i).start()
        y_copy(i).wait_send()

        @pl.when(i + AHEAD < pieces - 1)
        def _():
            y_copy(i + AHEAD).start()

        add(across, columns(i, y))

        @pl.when(i > 0)
        def _():
            fwd_arrival(i - 1).wait_recv()
            add(diagonal, columns(i - 1, y))

    def add_low(blocks, factors):
        @pl.loop(0, segs)
        def _(s):
            block, inner = s // seg_block, s % seg_block
            span_rows = pl.ds(pl.multiple_of(inner * seg_len, seg_len), seg_len)
            adapter = adapter_of(group, s)
            total = part[block % 2, block // 2, span_rows, :]
            for g, factor in zip(blocks, factors):
                cols = pl.ds(pl.multiple_of(g * 4 * tile + me * tile, tile), tile)
                total += jnp.dot(
                    t_all[block, span_rows, cols], factor(adapter, s),
                    preferred_element_type=jnp.float32,
                )
            part[block % 2, block // 2, span_rows, :] = total

    t_local.wait()
    w_local.wait()
    add_whole(me)

    @pl.loop(0, 4)
    def _(k):
        for way in range(2):
            one(way, k).wait_recv()
            two(way, k).start()

        @pl.when(k == 1)
        def _():
            remote(tok, t_all.at[sibling], pair_send, pair_recv, (group, sibling)).wait_recv()
            add_whole(sibling)

        @pl.when(k > 0)
        def _():
            take_piece(k - 1)

    d_local.wait()
    u_local.wait()

    @pl.loop(0, 4)
    def _(k):
        for way in range(2):
            two(way, k).wait_recv()
            three(way, k).start()
        take_piece(k + 3)

        @pl.when(k == 1)
        def _():
            add_low(
                [group, before, after],
                [lambda a, s: d_own[a], lambda a, s: d_one[0, a], lambda a, s: d_one[1, a]],
            )

    @pl.loop(0, segs)
    def _(s):
        for way in range(2):
            stage_three[way, s] = d_two[
                way, adapter_of(onward[way], s), pl.ds((1 - way) * half_tile, half_tile), :
            ]

    for way in range(2):
        three_picked(way).start()
    add_low(
        [at_place(place - 2), at_place(place + 2)],
        [lambda a, s: d_two[0, a], lambda a, s: d_two[1, a]],
    )

    @pl.loop(0, 2)
    def _(h):
        take_piece(h + 7)
        for j in range(2):
            for way in range(2):
                three(way, 2 * h + j).wait_recv()

    @pl.loop(0, segs)
    def _(s):
        for way in range(2):
            stage_four[way, s] = d_three[way, adapter_of(onward[way], s)]

    for way in range(2):
        four_picked(way).start()
    for way in range(2):
        u_copy(way, 0).start()
    take_piece(9)
    for way in range(2):
        three_picked(way).wait_recv()
    add_low(
        [at_place(place - 3), at_place(place + 3)],
        [
            lambda a, s: jnp.concatenate([d_three[0, a], d_three_picked[0, s]], axis=0),
            lambda a, s: jnp.concatenate([d_three_picked[1, s], d_three[1, a]], axis=0),
        ],
    )
    take_piece(10)
    for way in range(2):
        four_picked(way).wait_recv()
    add_low(
        [at_place(place + 4)],
        [lambda a, s: jnp.concatenate([d_four_picked[0, s], d_four_picked[1, s]], axis=0)],
    )

    hop1 = remote(part.at[1 - core], part_in, hop_send.at[0], hop_recv.at[0], (group, sibling))
    hop1.start()
    for way in range(2):
        u_arrival(way, 0).wait_recv()
        u_copy(way, 1).start()
    hop1.wait_recv()
    q0 = part[core, 0] + part_in[0]
    q1 = part[core, 1] + part_in[1]
    key_part = jnp.concatenate([q0[:, :rank], q1[:, :rank]], axis=1)
    value_part = jnp.concatenate([q0[:, rank:], q1[:, rank:]], axis=1)
    swap_out[0] = jnp.where(y == 0, value_part, key_part)
    swap_out[1] = jnp.where(y == 0, key_part, value_part)
    hop2 = remote(swap_out.at[0], swap_in, hop_send.at[1], hop_recv.at[1], (group, across))
    hop2.start()
    y_copy(pieces - 1).start()

    take_piece(11)
    for way in range(2):
        u_arrival(way, 1).wait_recv()
        u_copy(way, 2).start()
    take_piece(12)
    for way in range(2):
        u_arrival(way, 2).wait_recv()
        u_copy(way, 3).start()
    take_piece(13)
    for way in range(2):
        u_arrival(way, 3).wait_recv()

    total_rows = u_all.shape[0]
    index = lax.broadcasted_iota(jnp.int32, (1, total_rows), 1)
    by_group, by_adapter = up_rows.bit_length() - 1, up_rank.bit_length() - 1
    target = lax.shift_right_logical(index, by_group) * up_rank + (index & (up_rank - 1))
    holder = lax.shift_right_logical(index, by_adapter) & (adapters - 1)

    @pl.loop(0, segs)
    def _(s):
        yy = s // (2 * seg_block)
        line = lax.broadcasted_iota(jnp.int32, (double_rank, total_rows), 0)
        hit = (line == target + yy * rank) & (holder == adapter_of(group, s))
        pick = jnp.where(hit, 1.0, 0.0).astype(jnp.bfloat16)
        u_sel[s] = jnp.dot(pick, u_all[...], preferred_element_type=jnp.float32).astype(
            jnp.bfloat16
        )

    hop2.wait_recv()
    low[core] = (swap_out[1] + swap_in[...]).astype(jnp.bfloat16)
    hop3 = remote(low.at[core], low.at[core], hop_send.at[2], hop_recv.at[2], (group, sibling))
    hop3.start()
    take_piece(pieces - 2)
    remote(
        low.at[1 - core], low.at[1 - core], hop_send.at[2], hop_recv.at[2], (group, sibling)
    ).wait_recv()

    @pl.loop(0, segs)
    def _(s):
        block, inner = s // seg_block, s % seg_block
        span_rows = pl.ds(pl.multiple_of(inner * seg_len, seg_len), seg_len)
        acc[block, span_rows, :] += jnp.dot(
            low[block % 2, span_rows, :], u_sel[s], preferred_element_type=jnp.float32
        )

    out[me] = acc[me].astype(jnp.bfloat16)
    out[sibling] = acc[sibling].astype(jnp.bfloat16)
    take_piece(pieces - 1)
    out[across] = acc[across].astype(jnp.bfloat16)
    fwd_arrival(pieces - 1).wait_recv()
    add(diagonal, columns(pieces - 1, y))
    out[diagonal] = acc[diagonal].astype(jnp.bfloat16)

    pair.wait_send()
    hop1.wait_send()
    hop2.wait_send()
    hop3.wait_send()

    @pl.loop(0, pieces)
    def _(i):
        fwd_copy(i).wait_send()

    for way in range(2):
        for k in range(4):
            one(way, k).wait_send()
            two(way, k).wait_send()
            three(way, k).wait_send()
        three_picked(way).wait_send()
        four_picked(way).wait_send()
        for step in range(4):
            u_copy(way, step).wait_send()


def on_device(
    tokens,
    key_value_weight,
    adapter_down_weight,
    adapter_up_weight,
    adapter_per_request,
    request_per_segment,
):
    n_dp = lax.axis_size("dp")
    n_mp = lax.axis_size("mp")
    rows, depth = tokens.shape
    width = key_value_weight.shape[1]
    adapters, tile, double_rank = adapter_down_weight.shape
    up_rank = adapter_up_weight.shape[1]
    whole_tiles = tile % 256 == 0 and adapters % 4 == 0 and (adapters * up_rank) % 32 == 0
    powers = adapters & (adapters - 1) == 0 and up_rank & (up_rank - 1) == 0
    if n_mp != 4 or n_dp != 8 or not whole_tiles or not powers:
        return plain(
            tokens, key_value_weight, adapter_down_weight, adapter_up_weight,
            adapter_per_request, request_per_segment,
        )
    seg_group = request_per_segment.shape[0] // n_dp
    up_rows = adapters * up_rank
    bf16, f32 = jnp.bfloat16, jnp.float32
    dma = pltpu.SemaphoreType.DMA
    vmem = pl.BlockSpec(memory_space=pltpu.VMEM)
    result = pl.pallas_call(
        functools.partial(kernel, n_dp, up_rank),
        out_shape=jax.ShapeDtypeStruct((n_mp, rows, width), bf16),
        in_specs=[pl.BlockSpec(memory_space=pltpu.SMEM)] * 2
        + [pl.BlockSpec(memory_space=pl.ANY)] * 4,
        out_specs=vmem,
        scratch_shapes=[
            pltpu.VMEM((n_mp, rows, depth), bf16),
            pltpu.VMEM((depth, width), bf16),
            pltpu.VMEM((adapters, tile, double_rank), bf16),
            pltpu.VMEM((2, adapters, tile, double_rank), bf16),
            pltpu.VMEM((2, adapters, tile, double_rank), bf16),
            pltpu.VMEM((2, adapters, tile // 2, double_rank), bf16),
            pltpu.VMEM((2, seg_group, tile // 2, double_rank), bf16),
            pltpu.VMEM((2, seg_group, tile // 2, double_rank), bf16),
            pltpu.VMEM((2, seg_group, tile // 2, double_rank), bf16),
            pltpu.VMEM((2, seg_group, tile // 2, double_rank), bf16),
            pltpu.VMEM((n_dp * up_rows, width), bf16),
            pltpu.VMEM((n_mp, rows, width), f32),
            pltpu.VMEM((2, 2, rows, double_rank), f32),
            pltpu.VMEM((2, rows, double_rank), f32),
            pltpu.VMEM((2, rows, double_rank), f32),
            pltpu.VMEM((rows, double_rank), f32),
            pltpu.VMEM((2, rows, double_rank), bf16),
            pltpu.VMEM((seg_group, double_rank, width), bf16),
            dma((4,)),
            dma,
            dma,
            dma((2 * n_dp,)),
            dma((2 * n_dp,)),
            dma((2 * n_dp,)),
            dma((2 * n_dp,)),
            dma((2, 14)),
            dma((2, 14)),
            dma((2, 4)),
            dma((2, 4)),
            dma((3,)),
            dma((3,)),
        ],
        compiler_params=pltpu.CompilerParams(
            collective_id=0, has_side_effects=True, vmem_limit_bytes=63 * 2**20
        ),
    )(
        adapter_per_request, request_per_segment, tokens, key_value_weight, adapter_down_weight,
        adapter_up_weight.reshape(up_rows, width),
    )
    return result.reshape(n_mp * rows, width)


def solution(mesh):
    placed = (
        P(("dp", "mp"), None),
        P(None, "mp"),
        P(None, ("dp", "mp"), None),
        P(None, "dp", "mp"),
        P(),
        P(),
    )
    return jax.shard_map(
        on_device, mesh=mesh, in_specs=placed, out_specs=P("dp", "mp"), check_vma=False
    )
```

```python
import functools

import jax
import jax.numpy as jnp
from jax import lax
from jax.experimental import pallas as pl
from jax.experimental.pallas import tpu as pltpu
from jax.sharding import PartitionSpec as P

MESH = pl.DeviceIdType.MESH
AHEAD = 6
PARTS = 4


def plain(
    tokens,
    key_value_weight,
    adapter_down_weight,
    adapter_up_weight,
    adapter_per_request,
    request_per_segment,
):
    n_dp = lax.axis_size("dp")
    n_mp = lax.axis_size("mp")
    group = lax.axis_index("dp")
    column = lax.axis_index("mp")
    seg_total = request_per_segment.shape[0]
    seg_group = seg_total // n_dp
    seg_adapter = jnp.take(adapter_per_request, request_per_segment, axis=0)
    local_portion = lax.dynamic_slice_in_dim(seg_adapter, group * seg_group, seg_group)
    gathered = lax.all_gather(tokens, "mp", axis=0, tiled=True)
    rows = gathered.shape[0]
    seg_len = rows // seg_group
    width_tile = adapter_down_weight.shape[1]
    double_rank = adapter_down_weight.shape[2]
    rank = double_rank // 2
    column_tile = adapter_up_weight.shape[2]
    base = jnp.dot(gathered, key_value_weight, preferred_element_type=jnp.float32)
    strided = lax.dynamic_index_in_dim(
        gathered.reshape(rows, n_dp, n_mp, width_tile), column, 2, keepdims=False
    ).reshape(seg_group, seg_len, n_dp * width_tile)
    selected_factor = jnp.take(
        lax.all_gather(adapter_down_weight, "dp", axis=1, tiled=True), local_portion, axis=0
    )
    partial_low = jnp.einsum(
        "sti,sir->str", strided, selected_factor, preferred_element_type=jnp.float32
    )
    selected_factor = jnp.take(
        lax.all_gather(adapter_up_weight, "dp", axis=1, tiled=True), local_portion, axis=0
    )
    rank_output = lax.psum(partial_low, "mp").astype(jnp.bfloat16)
    key_width = n_mp * column_tile // 2
    half = column * column_tile // key_width
    low_half = lax.dynamic_slice_in_dim(rank_output, half * rank, rank, 2)
    delta = jnp.einsum(
        "str,src->stc", low_half, selected_factor, preferred_element_type=jnp.float32
    )
    return (base + delta.reshape(rows, column_tile)).astype(jnp.bfloat16)


def kernel(
    n_dp,
    up_rank,
    requests_in,
    segments_in,
    tok,
    weight,
    down,
    up,
    out,
    requests,
    segments,
    t_all,
    w_all,
    d_own,
    d_one,
    d_two,
    d_three,
    d_three_picked,
    d_four_picked,
    stage_three,
    stage_four,
    u_all,
    acc,
    part,
    part_in,
    swap_out,
    swap_in,
    low,
    u_sel,
    local_sem,
    pair_send,
    pair_recv,
    y_send,
    y_recv,
    fwd_send,
    fwd_recv,
    d_send,
    d_recv,
    u_send,
    u_recv,
    hop_send,
    hop_recv,
):
    group = lax.axis_index("dp")
    me = lax.axis_index("mp")
    y, core = me // 2, me % 2
    other_y = 1 - y
    sibling = y * 2 + (1 - core)
    across = other_y * 2 + core
    diagonal = other_y * 2 + (1 - core)

    rows, depth = tok.shape
    adapters, tile, double_rank = down.shape
    rank = double_rank // 2
    up_rows = up.shape[0]
    pieces = 2 * n_dp
    piece = 2 * tile
    span = n_dp // 2
    half_tile = tile // 2
    quarter = adapters // 4
    segs = segments.shape[0] // n_dp
    seg_block = segs // 4
    seg_len = rows // seg_block

    z, x = group // 2, group % 2
    place = z + x * (n_dp - 1 - 2 * z)

    def at_place(q):
        q = (q + 2 * n_dp) % n_dp
        side, step = q // span, q % span
        return (step + side * (span - 1 - 2 * step)) * 2 + side

    after, before = at_place(place + 1), at_place(place - 1)
    onward = (after, before)

    def adapter_of(g, seg):
        return requests[segments[g * segs + seg]]

    barrier = pltpu.get_barrier_semaphore()
    for partner in ((after, me), (before, me), (group, across), (group, sibling)):
        pl.semaphore_signal(barrier, inc=1, device_id=partner, device_id_type=MESH)
    pl.semaphore_wait(barrier, 4)

    def remote(src, dst, send, recv, partner):
        return pltpu.make_async_remote_copy(
            src_ref=src, dst_ref=dst, send_sem=send, recv_sem=recv,
            device_id=partner, device_id_type=MESH,
        )

    def quarter_of(k):
        return pl.ds(k * quarter, quarter)

    def one(way, k):
        return remote(
            down.at[quarter_of(k)], d_one.at[way, quarter_of(k)],
            d_send.at[way, k], d_recv.at[way, k], (onward[way], me),
        )

    def two(way, k):
        return remote(
            d_one.at[way, quarter_of(k)], d_two.at[way, quarter_of(k)],
            d_send.at[way, 4 + k], d_recv.at[way, 4 + k], (onward[way], me),
        )

    def three(way, k):
        return remote(
            d_two.at[way, quarter_of(k), pl.ds(way * half_tile, half_tile)],
            d_three.at[way, quarter_of(k)],
            d_send.at[way, 8 + k], d_recv.at[way, 8 + k], (onward[way], me),
        )

    def three_picked(way):
        return remote(
            stage_three.at[way], d_three_picked.at[way],
            d_send.at[way, 12], d_recv.at[way, 12], (onward[way], me),
        )

    def four_picked(way):
        return remote(
            stage_four.at[way], d_four_picked.at[way],
            d_send.at[way, 13], d_recv.at[way, 13], (onward[way], me),
        )

    def u_rows(way, step, block):
        if step < span - 1:
            return pl.ds(pl.multiple_of(block * up_rows, up_rows), up_rows)
        half = up_rows // 2
        return pl.ds(pl.multiple_of(block * up_rows + way * half, half), half)

    def u_copy(way, step):
        block = at_place(place - step) if way == 0 else at_place(place + step)
        there = u_rows(way, step, block)
        return remote(
            up if step == 0 else u_all.at[there], u_all.at[there],
            u_send.at[way, step], u_recv.at[way, step], (onward[way], me),
        )

    def u_arrival(way, step):
        block = at_place(place - 1 - step) if way == 0 else at_place(place + 1 + step)
        there = u_rows(way, step, block)
        return remote(
            u_all.at[there], u_all.at[there],
            u_send.at[way, step], u_recv.at[way, step], (onward[way], me),
        )

    def near(k):
        return at_place(place + (k + 1) // 2 * (1 - 2 * (k % 2)))

    def columns(i, side):
        part_of = i - (pieces - 1)
        if isinstance(i, int) and part_of >= 0:
            width = piece // PARTS
            start = near(n_dp - 1) * (4 * tile) + ((side + 1) % 2) * piece + part_of * width
            return pl.ds(pl.multiple_of(start, width), width)
        start = near(i % n_dp) * (4 * tile) + ((side + i // n_dp) % 2) * piece
        return pl.ds(pl.multiple_of(start, piece), piece)

    def y_copy(i):
        cols = columns(i, other_y)
        return remote(
            tok.at[:, cols], t_all.at[me, :, cols], y_send.at[i], y_recv.at[i], (group, across)
        )

    def y_arrival(i):
        cols = columns(i, y)
        return remote(
            tok.at[:, cols], t_all.at[across, :, cols], y_send.at[i], y_recv.at[i],
            (group, across),
        )

    def fwd_copy(i):
        cols = columns(i, y)
        return remote(
            t_all.at[across, :, cols], t_all.at[across, :, cols],
            fwd_send.at[i], fwd_recv.at[i], (group, sibling),
        )

    def fwd_arrival(i):
        cols = columns(i, y)
        return remote(
            t_all.at[diagonal, :, cols], t_all.at[diagonal, :, cols],
            fwd_send.at[i], fwd_recv.at[i], (group, sibling),
        )

    for i in range(AHEAD):
        y_copy(i).start()
    for k in range(4):
        for way in range(2):
            one(way, k).start()
    t_local = pltpu.make_async_copy(tok, t_all.at[me], local_sem.at[0])
    w_local = pltpu.make_async_copy(weight, w_all, local_sem.at[1])
    d_local = pltpu.make_async_copy(down, d_own, local_sem.at[2])
    u_local = pltpu.make_async_copy(
        up, u_all.at[pl.ds(pl.multiple_of(group * up_rows, up_rows), up_rows)], local_sem.at[3]
    )
    r_local = pltpu.make_async_copy(requests_in, requests, local_sem.at[4])
    s_local = pltpu.make_async_copy(segments_in, segments, local_sem.at[5])
    r_local.start()
    s_local.start()
    t_local.start()
    w_local.start()
    d_local.start()
    u_local.start()
    pair = remote(tok, t_all.at[me], pair_send, pair_recv, (group, sibling))
    pair.start()

    acc[...] = jnp.zeros_like(acc)
    part[...] = jnp.zeros_like(part)

    def add(block, cols):
        acc[block] += jnp.dot(
            t_all[block, :, cols], w_all[cols, :], preferred_element_type=jnp.float32
        )

    def add_whole(block):
        @pl.loop(0, n_dp)
        def _(k):
            add(block, pl.ds(pl.multiple_of(k * 4 * tile, 4 * tile), 4 * tile))

    def take_piece(i):
        y_arrival(i).wait_recv()
        fwd_copy(i).start()
        y_copy(i).wait_send()

        @pl.when(i + AHEAD < pieces - 1)
        def _():
            y_copy(i + AHEAD).start()

        add(across, columns(i, y))

        @pl.when(i > 0)
        def _():
            fwd_arrival(i - 1).wait_recv()
            add(diagonal, columns(i - 1, y))

    def add_low(blocks, factors):
        @pl.loop(0, segs)
        def _(s):
            block, inner = s // seg_block, s % seg_block
            span_rows = pl.ds(pl.multiple_of(inner * seg_len, seg_len), seg_len)
            adapter = adapter_of(group, s)
            total = part[block % 2, block // 2, span_rows, :]
            for g, factor in zip(blocks, factors):
                cols = pl.ds(pl.multiple_of(g * 4 * tile + me * tile, tile), tile)
                total += jnp.dot(
                    t_all[block, span_rows, cols], factor(adapter, s),
                    preferred_element_type=jnp.float32,
                )
            part[block % 2, block // 2, span_rows, :] = total

    t_local.wait()
    w_local.wait()
    add_whole(me)

    @pl.loop(0, 4)
    def _(k):
        for way in range(2):
            one(way, k).wait_recv()
            two(way, k).start()

        @pl.when(k == 1)
        def _():
            remote(tok, t_all.at[sibling], pair_send, pair_recv, (group, sibling)).wait_recv()
            add_whole(sibling)

        @pl.when(k > 0)
        def _():
            take_piece(k - 1)

    d_local.wait()
    u_local.wait()
    r_local.wait()
    s_local.wait()

    @pl.loop(0, 4)
    def _(k):
        for way in range(2):
            two(way, k).wait_recv()
            three(way, k).start()
        take_piece(k + 3)

        @pl.when(k == 1)
        def _():
            add_low(
                [group, before, after],
                [lambda a, s: d_own[a], lambda a, s: d_one[0, a], lambda a, s: d_one[1, a]],
            )

    @pl.loop(0, segs)
    def _(s):
        for way in range(2):
            stage_three[way, s] = d_two[
                way, adapter_of(onward[way], s), pl.ds((1 - way) * half_tile, half_tile), :
            ]

    for way in range(2):
        three_picked(way).start()
    add_low(
        [at_place(place - 2), at_place(place + 2)],
        [lambda a, s: d_two[0, a], lambda a, s: d_two[1, a]],
    )

    @pl.loop(0, 2)
    def _(h):
        take_piece(h + 7)
        for j in range(2):
            for way in range(2):
                three(way, 2 * h + j).wait_recv()

    @pl.loop(0, segs)
    def _(s):
        for way in range(2):
            stage_four[way, s] = d_three[way, adapter_of(onward[way], s)]

    for way in range(2):
        four_picked(way).start()
    for way in range(2):
        u_copy(way, 0).start()
    take_piece(9)
    for way in range(2):
        three_picked(way).wait_recv()
    add_low(
        [at_place(place - 3), at_place(place + 3)],
        [
            lambda a, s: jnp.concatenate([d_three[0, a], d_three_picked[0, s]], axis=0),
            lambda a, s: jnp.concatenate([d_three_picked[1, s], d_three[1, a]], axis=0),
        ],
    )
    take_piece(10)
    for way in range(2):
        four_picked(way).wait_recv()
    add_low(
        [at_place(place + 4)],
        [lambda a, s: jnp.concatenate([d_four_picked[0, s], d_four_picked[1, s]], axis=0)],
    )

    hop1 = remote(part.at[1 - core], part_in, hop_send.at[0], hop_recv.at[0], (group, sibling))
    hop1.start()
    for way in range(2):
        u_arrival(way, 0).wait_recv()
        u_copy(way, 1).start()
    hop1.wait_recv()
    q0 = part[core, 0] + part_in[0]
    q1 = part[core, 1] + part_in[1]
    key_part = jnp.concatenate([q0[:, :rank], q1[:, :rank]], axis=1)
    value_part = jnp.concatenate([q0[:, rank:], q1[:, rank:]], axis=1)
    swap_out[0] = jnp.where(y == 0, value_part, key_part)
    swap_out[1] = jnp.where(y == 0, key_part, value_part)
    hop2 = remote(swap_out.at[0], swap_in, hop_send.at[1], hop_recv.at[1], (group, across))
    hop2.start()
    for i in range(pieces - 1, pieces - 1 + PARTS):
        y_copy(i).start()

    take_piece(11)
    for way in range(2):
        u_arrival(way, 1).wait_recv()
        u_copy(way, 2).start()
    take_piece(12)
    for way in range(2):
        u_arrival(way, 2).wait_recv()
        u_copy(way, 3).start()
    take_piece(13)
    for way in range(2):
        u_arrival(way, 3).wait_recv()

    total_rows = u_all.shape[0]
    index = lax.broadcasted_iota(jnp.int32, (1, total_rows), 1)
    by_group, by_adapter = up_rows.bit_length() - 1, up_rank.bit_length() - 1
    target = lax.shift_right_logical(index, by_group) * up_rank + (index & (up_rank - 1))
    holder = lax.shift_right_logical(index, by_adapter) & (adapters - 1)

    @pl.loop(0, segs)
    def _(s):
        yy = s // (2 * seg_block)
        line = lax.broadcasted_iota(jnp.int32, (double_rank, total_rows), 0)
        hit = (line == target + yy * rank) & (holder == adapter_of(group, s))
        pick = jnp.where(hit, 1.0, 0.0).astype(jnp.bfloat16)
        u_sel[s] = jnp.dot(pick, u_all[...], preferred_element_type=jnp.float32).astype(
            jnp.bfloat16
        )

    hop2.wait_recv()
    low[core] = (swap_out[1] + swap_in[...]).astype(jnp.bfloat16)
    hop3 = remote(low.at[core], low.at[core], hop_send.at[2], hop_recv.at[2], (group, sibling))
    hop3.start()
    take_piece(pieces - 2)
    remote(
        low.at[1 - core], low.at[1 - core], hop_send.at[2], hop_recv.at[2], (group, sibling)
    ).wait_recv()

    @pl.loop(0, segs)
    def _(s):
        block, inner = s // seg_block, s % seg_block
        span_rows = pl.ds(pl.multiple_of(inner * seg_len, seg_len), seg_len)
        acc[block, span_rows, :] += jnp.dot(
            low[block % 2, span_rows, :], u_sel[s], preferred_element_type=jnp.float32
        )

    out[me] = acc[me].astype(jnp.bfloat16)
    out[sibling] = acc[sibling].astype(jnp.bfloat16)

    pair.wait_send()
    hop1.wait_send()
    hop2.wait_send()
    hop3.wait_send()
    for way in range(2):
        for k in range(4):
            one(way, k).wait_send()
            two(way, k).wait_send()
            three(way, k).wait_send()
        three_picked(way).wait_send()
        four_picked(way).wait_send()
        for step in range(4):
            u_copy(way, step).wait_send()

    @pl.loop(0, pieces - 2)
    def _(i):
        fwd_copy(i).wait_send()

    fwd_arrival(pieces - 2).wait_recv()
    add(diagonal, columns(pieces - 2, y))

    tail = range(pieces - 1, pieces - 1 + PARTS)
    for i in tail:
        y_arrival(i).wait_recv()
        fwd_copy(i).start()
    whole = pl.ds(pl.multiple_of(near(n_dp - 1) * (4 * tile) + other_y * piece, piece), piece)
    add(across, whole)
    out[across] = acc[across].astype(jnp.bfloat16)
    for i in tail:
        fwd_arrival(i).wait_recv()
    add(diagonal, whole)
    out[diagonal] = acc[diagonal].astype(jnp.bfloat16)
    for i in tail:
        y_copy(i).wait_send()
    for i in range(pieces - 2, pieces - 1 + PARTS):
        fwd_copy(i).wait_send()


def on_device(
    tokens,
    key_value_weight,
    adapter_down_weight,
    adapter_up_weight,
    adapter_per_request,
    request_per_segment,
):
    n_dp = lax.axis_size("dp")
    n_mp = lax.axis_size("mp")
    rows, depth = tokens.shape
    width = key_value_weight.shape[1]
    adapters, tile, double_rank = adapter_down_weight.shape
    up_rank = adapter_up_weight.shape[1]
    whole_tiles = tile % 256 == 0 and adapters % 4 == 0 and (adapters * up_rank) % 32 == 0
    powers = adapters & (adapters - 1) == 0 and up_rank & (up_rank - 1) == 0
    if n_mp != 4 or n_dp != 8 or not whole_tiles or not powers:
        return plain(
            tokens, key_value_weight, adapter_down_weight, adapter_up_weight,
            adapter_per_request, request_per_segment,
        )
    seg_group = request_per_segment.shape[0] // n_dp
    up_rows = adapters * up_rank
    bf16, f32 = jnp.bfloat16, jnp.float32
    dma = pltpu.SemaphoreType.DMA
    vmem = pl.BlockSpec(memory_space=pltpu.VMEM)
    result = pl.pallas_call(
        functools.partial(kernel, n_dp, up_rank),
        out_shape=jax.ShapeDtypeStruct((n_mp, rows, width), bf16),
        in_specs=[pl.BlockSpec(memory_space=pltpu.HBM)] * 6,
        out_specs=vmem,
        scratch_shapes=[
            pltpu.SMEM(adapter_per_request.shape, jnp.int32),
            pltpu.SMEM(request_per_segment.shape, jnp.int32),
            pltpu.VMEM((n_mp, rows, depth), bf16),
            pltpu.VMEM((depth, width), bf16),
            pltpu.VMEM((adapters, tile, double_rank), bf16),
            pltpu.VMEM((2, adapters, tile, double_rank), bf16),
            pltpu.VMEM((2, adapters, tile, double_rank), bf16),
            pltpu.VMEM((2, adapters, tile // 2, double_rank), bf16),
            pltpu.VMEM((2, seg_group, tile // 2, double_rank), bf16),
            pltpu.VMEM((2, seg_group, tile // 2, double_rank), bf16),
            pltpu.VMEM((2, seg_group, tile // 2, double_rank), bf16),
            pltpu.VMEM((2, seg_group, tile // 2, double_rank), bf16),
            pltpu.VMEM((n_dp * up_rows, width), bf16),
            pltpu.VMEM((n_mp, rows, width), f32),
            pltpu.VMEM((2, 2, rows, double_rank), f32),
            pltpu.VMEM((2, rows, double_rank), f32),
            pltpu.VMEM((2, rows, double_rank), f32),
            pltpu.VMEM((rows, double_rank), f32),
            pltpu.VMEM((2, rows, double_rank), bf16),
            pltpu.VMEM((seg_group, double_rank, width), bf16),
            dma((6,)),
            dma,
            dma,
            dma((2 * n_dp + PARTS - 1,)),
            dma((2 * n_dp + PARTS - 1,)),
            dma((2 * n_dp + PARTS - 1,)),
            dma((2 * n_dp + PARTS - 1,)),
            dma((2, 14)),
            dma((2, 14)),
            dma((2, 4)),
            dma((2, 4)),
            dma((3,)),
            dma((3,)),
        ],
        compiler_params=pltpu.CompilerParams(
            collective_id=0, has_side_effects=True, vmem_limit_bytes=52 * 2**20
        ),
    )(
        *(
            pltpu.with_memory_space_constraint(a, pltpu.HBM)
            for a in (
                adapter_per_request, request_per_segment, tokens, key_value_weight,
                adapter_down_weight, adapter_up_weight.reshape(up_rows, width),
            )
        )
    )
    return result.reshape(n_mp * rows, width)


def solution(mesh):
    placed = (
        P(("dp", "mp"), None),
        P(None, "mp"),
        P(None, ("dp", "mp"), None),
        P(None, "dp", "mp"),
        P(),
        P(),
    )
    return jax.shard_map(
        on_device, mesh=mesh, in_specs=placed, out_specs=P("dp", "mp"), check_vma=False
    )
```

```python
import functools

import jax
import jax.numpy as jnp
from jax import lax
from jax.experimental import pallas as pl
from jax.experimental.pallas import tpu as pltpu
from jax.sharding import PartitionSpec as P

MESH = pl.DeviceIdType.MESH
AHEAD = 6
PARTS = 4


def plain(
    tokens,
    key_value_weight,
    adapter_down_weight,
    adapter_up_weight,
    adapter_per_request,
    request_per_segment,
):
    n_dp = lax.axis_size("dp")
    n_mp = lax.axis_size("mp")
    group = lax.axis_index("dp")
    column = lax.axis_index("mp")
    seg_total = request_per_segment.shape[0]
    seg_group = seg_total // n_dp
    seg_adapter = jnp.take(adapter_per_request, request_per_segment, axis=0)
    local_portion = lax.dynamic_slice_in_dim(seg_adapter, group * seg_group, seg_group)
    gathered = lax.all_gather(tokens, "mp", axis=0, tiled=True)
    rows = gathered.shape[0]
    seg_len = rows // seg_group
    width_tile = adapter_down_weight.shape[1]
    double_rank = adapter_down_weight.shape[2]
    rank = double_rank // 2
    column_tile = adapter_up_weight.shape[2]
    base = jnp.dot(gathered, key_value_weight, preferred_element_type=jnp.float32)
    strided = lax.dynamic_index_in_dim(
        gathered.reshape(rows, n_dp, n_mp, width_tile), column, 2, keepdims=False
    ).reshape(seg_group, seg_len, n_dp * width_tile)
    selected_factor = jnp.take(
        lax.all_gather(adapter_down_weight, "dp", axis=1, tiled=True), local_portion, axis=0
    )
    partial_low = jnp.einsum(
        "sti,sir->str", strided, selected_factor, preferred_element_type=jnp.float32
    )
    selected_factor = jnp.take(
        lax.all_gather(adapter_up_weight, "dp", axis=1, tiled=True), local_portion, axis=0
    )
    rank_output = lax.psum(partial_low, "mp").astype(jnp.bfloat16)
    key_width = n_mp * column_tile // 2
    half = column * column_tile // key_width
    low_half = lax.dynamic_slice_in_dim(rank_output, half * rank, rank, 2)
    delta = jnp.einsum(
        "str,src->stc", low_half, selected_factor, preferred_element_type=jnp.float32
    )
    return (base + delta.reshape(rows, column_tile)).astype(jnp.bfloat16)


def kernel(
    n_dp,
    up_rank,
    requests_in,
    segments_in,
    tok,
    weight,
    down,
    up,
    out,
    requests,
    segments,
    t_all,
    w_all,
    d_own,
    d_one,
    d_two,
    d_three,
    d_three_picked,
    d_four_picked,
    stage_three,
    stage_four,
    u_all,
    acc,
    part,
    part_in,
    kept,
    swap_out,
    swap_in,
    low,
    u_sel,
    local_sem,
    pair_send,
    pair_recv,
    y_send,
    y_recv,
    fwd_send,
    fwd_recv,
    d_send,
    d_recv,
    u_send,
    u_recv,
    hop_send,
    hop_recv,
):
    group = lax.axis_index("dp")
    me = lax.axis_index("mp")
    y, core = me // 2, me % 2
    other_y = 1 - y
    sibling = y * 2 + (1 - core)
    across = other_y * 2 + core
    diagonal = other_y * 2 + (1 - core)

    rows, depth = tok.shape
    adapters, tile, double_rank = down.shape
    rank = double_rank // 2
    up_rows = up.shape[0]
    pieces = 2 * n_dp
    piece = 2 * tile
    span = n_dp // 2
    half_tile = tile // 2
    quarter = adapters // 4
    segs = segments.shape[0] // n_dp
    seg_block = segs // 4
    seg_len = rows // seg_block

    z, x = group // 2, group % 2
    place = z + x * (n_dp - 1 - 2 * z)

    def at_place(q):
        q = (q + 2 * n_dp) % n_dp
        side, step = q // span, q % span
        return (step + side * (span - 1 - 2 * step)) * 2 + side

    after, before = at_place(place + 1), at_place(place - 1)
    onward = (after, before)

    def adapter_of(g, seg):
        return requests[segments[g * segs + seg]]

    barrier = pltpu.get_barrier_semaphore()
    for partner in ((after, me), (before, me), (group, across), (group, sibling)):
        pl.semaphore_signal(barrier, inc=1, device_id=partner, device_id_type=MESH)
    pl.semaphore_wait(barrier, 4)

    def remote(src, dst, send, recv, partner):
        return pltpu.make_async_remote_copy(
            src_ref=src, dst_ref=dst, send_sem=send, recv_sem=recv,
            device_id=partner, device_id_type=MESH,
        )

    def quarter_of(k):
        return pl.ds(k * quarter, quarter)

    def one(way, k):
        return remote(
            down.at[quarter_of(k)], d_one.at[way, quarter_of(k)],
            d_send.at[way, k], d_recv.at[way, k], (onward[way], me),
        )

    def two(way, k):
        return remote(
            d_one.at[way, quarter_of(k)], d_two.at[way, quarter_of(k)],
            d_send.at[way, 4 + k], d_recv.at[way, 4 + k], (onward[way], me),
        )

    def three(way, k):
        return remote(
            d_two.at[way, quarter_of(k), pl.ds(way * half_tile, half_tile)],
            d_three.at[way, quarter_of(k)],
            d_send.at[way, 8 + k], d_recv.at[way, 8 + k], (onward[way], me),
        )

    def three_picked(way):
        return remote(
            stage_three.at[way], d_three_picked.at[way],
            d_send.at[way, 12], d_recv.at[way, 12], (onward[way], me),
        )

    def four_picked(way):
        return remote(
            stage_four.at[way], d_four_picked.at[way],
            d_send.at[way, 13], d_recv.at[way, 13], (onward[way], me),
        )

    def u_rows(way, step, block):
        if step < span - 1:
            return pl.ds(pl.multiple_of(block * up_rows, up_rows), up_rows)
        half = up_rows // 2
        return pl.ds(pl.multiple_of(block * up_rows + way * half, half), half)

    def u_copy(way, step):
        block = at_place(place - step) if way == 0 else at_place(place + step)
        there = u_rows(way, step, block)
        return remote(
            up if step == 0 else u_all.at[there], u_all.at[there],
            u_send.at[way, step], u_recv.at[way, step], (onward[way], me),
        )

    def u_arrival(way, step):
        block = at_place(place - 1 - step) if way == 0 else at_place(place + 1 + step)
        there = u_rows(way, step, block)
        return remote(
            u_all.at[there], u_all.at[there],
            u_send.at[way, step], u_recv.at[way, step], (onward[way], me),
        )

    def near(k):
        return at_place(place + (k + 1) // 2 * (1 - 2 * (k % 2)))

    def columns(i, side):
        part_of = i - (pieces - 1)
        if isinstance(i, int) and part_of >= 0:
            width = piece // PARTS
            start = near(n_dp - 1) * (4 * tile) + ((side + 1) % 2) * piece + part_of * width
            return pl.ds(pl.multiple_of(start, width), width)
        start = near(i % n_dp) * (4 * tile) + ((side + i // n_dp) % 2) * piece
        return pl.ds(pl.multiple_of(start, piece), piece)

    def y_copy(i):
        cols = columns(i, other_y)
        return remote(
            tok.at[:, cols], t_all.at[me, :, cols], y_send.at[i], y_recv.at[i], (group, across)
        )

    def y_arrival(i):
        cols = columns(i, y)
        return remote(
            tok.at[:, cols], t_all.at[across, :, cols], y_send.at[i], y_recv.at[i],
            (group, across),
        )

    def fwd_copy(i):
        cols = columns(i, y)
        return remote(
            t_all.at[across, :, cols], t_all.at[across, :, cols],
            fwd_send.at[i], fwd_recv.at[i], (group, sibling),
        )

    def fwd_arrival(i):
        cols = columns(i, y)
        return remote(
            t_all.at[diagonal, :, cols], t_all.at[diagonal, :, cols],
            fwd_send.at[i], fwd_recv.at[i], (group, sibling),
        )

    for i in range(AHEAD):
        y_copy(i).start()
    for k in range(4):
        for way in range(2):
            one(way, k).start()
    for way in range(2):
        u_copy(way, 0).start()
    t_local = pltpu.make_async_copy(tok, t_all.at[me], local_sem.at[0])
    w_local = pltpu.make_async_copy(weight, w_all, local_sem.at[1])
    d_local = pltpu.make_async_copy(down, d_own, local_sem.at[2])
    u_local = pltpu.make_async_copy(
        up, u_all.at[pl.ds(pl.multiple_of(group * up_rows, up_rows), up_rows)], local_sem.at[3]
    )
    r_local = pltpu.make_async_copy(requests_in, requests, local_sem.at[4])
    s_local = pltpu.make_async_copy(segments_in, segments, local_sem.at[5])
    r_local.start()
    s_local.start()
    t_local.start()
    w_local.start()
    d_local.start()
    u_local.start()
    pair = remote(tok, t_all.at[me], pair_send, pair_recv, (group, sibling))
    pair.start()

    acc[...] = jnp.zeros_like(acc)
    part[...] = jnp.zeros_like(part)

    def add(block, cols):
        acc[block] += jnp.dot(
            t_all[block, :, cols], w_all[cols, :], preferred_element_type=jnp.float32
        )

    def add_whole(block):
        @pl.loop(0, n_dp)
        def _(k):
            add(block, pl.ds(pl.multiple_of(k * 4 * tile, 4 * tile), 4 * tile))

    def take_piece(i):
        y_arrival(i).wait_recv()
        fwd_copy(i).start()
        y_copy(i).wait_send()

        @pl.when(i + AHEAD < pieces - 1)
        def _():
            y_copy(i + AHEAD).start()

        add(across, columns(i, y))

        @pl.when(i > 0)
        def _():
            fwd_arrival(i - 1).wait_recv()
            add(diagonal, columns(i - 1, y))

    def add_low(blocks, factors):
        @pl.loop(0, segs)
        def _(s):
            block, inner = s // seg_block, s % seg_block
            span_rows = pl.ds(pl.multiple_of(inner * seg_len, seg_len), seg_len)
            adapter = adapter_of(group, s)
            total = part[block % 2, block // 2, span_rows, :]
            for g, factor in zip(blocks, factors):
                cols = pl.ds(pl.multiple_of(g * 4 * tile + me * tile, tile), tile)
                total += jnp.dot(
                    t_all[block, span_rows, cols], factor(adapter, s),
                    preferred_element_type=jnp.float32,
                )
            part[block % 2, block // 2, span_rows, :] = total

    t_local.wait()
    w_local.wait()
    add_whole(me)

    @pl.loop(0, 4)
    def _(k):
        for way in range(2):
            one(way, k).wait_recv()
            two(way, k).start()

        @pl.when(k == 1)
        def _():
            remote(tok, t_all.at[sibling], pair_send, pair_recv, (group, sibling)).wait_recv()
            add_whole(sibling)

        @pl.when(k > 0)
        def _():
            take_piece(k - 1)

    for way in range(2):
        u_arrival(way, 0).wait_recv()
        u_copy(way, 1).start()
    d_local.wait()
    u_local.wait()
    r_local.wait()
    s_local.wait()

    @pl.loop(0, 4)
    def _(k):
        for way in range(2):
            two(way, k).wait_recv()
            three(way, k).start()
        take_piece(k + 3)

        @pl.when(k == 1)
        def _():
            add_low(
                [group, before, after],
                [lambda a, s: d_own[a], lambda a, s: d_one[0, a], lambda a, s: d_one[1, a]],
            )

    @pl.loop(0, segs)
    def _(s):
        for way in range(2):
            stage_three[way, s] = d_two[
                way, adapter_of(onward[way], s), pl.ds((1 - way) * half_tile, half_tile), :
            ]

    for way in range(2):
        three_picked(way).start()
    add_low(
        [at_place(place - 2), at_place(place + 2)],
        [lambda a, s: d_two[0, a], lambda a, s: d_two[1, a]],
    )

    @pl.loop(0, 2)
    def _(h):
        take_piece(h + 7)
        for j in range(2):
            for way in range(2):
                three(way, 2 * h + j).wait_recv()

    @pl.loop(0, segs)
    def _(s):
        for way in range(2):
            stage_four[way, s] = d_three[way, adapter_of(onward[way], s)]

    for way in range(2):
        four_picked(way).start()
    for way in range(2):
        u_arrival(way, 1).wait_recv()
        u_copy(way, 2).start()
    take_piece(9)
    for i in range(pieces - 1, pieces - 1 + PARTS // 2):
        y_copy(i).start()
    for way in range(2):
        three_picked(way).wait_recv()
    add_low(
        [at_place(place - 3), at_place(place + 3)],
        [
            lambda a, s: jnp.concatenate([d_three[0, a], d_three_picked[0, s]], axis=0),
            lambda a, s: jnp.concatenate([d_three_picked[1, s], d_three[1, a]], axis=0),
        ],
    )
    take_piece(10)
    for way in range(2):
        four_picked(way).wait_recv()
    add_low(
        [at_place(place + 4)],
        [lambda a, s: jnp.concatenate([d_four_picked[0, s], d_four_picked[1, s]], axis=0)],
    )

    hop1 = remote(part.at[1 - core], part_in, hop_send.at[0], hop_recv.at[0], (group, sibling))
    hop1.start()
    hop1.wait_recv()
    q0 = part[core, 0] + part_in[0]
    q1 = part[core, 1] + part_in[1]
    key_part = jnp.concatenate([q0[:, :rank], q1[:, :rank]], axis=1)
    value_part = jnp.concatenate([q0[:, rank:], q1[:, rank:]], axis=1)
    swap_out[...] = jnp.where(y == 0, value_part, key_part).astype(jnp.bfloat16)
    kept[...] = jnp.where(y == 0, key_part, value_part)
    hop2 = remote(swap_out, swap_in, hop_send.at[1], hop_recv.at[1], (group, across))
    hop2.start()
    for i in range(pieces - 1 + PARTS // 2, pieces - 1 + PARTS):
        y_copy(i).start()
    for way in range(2):
        u_arrival(way, 2).wait_recv()
        u_copy(way, 3).start()

    take_piece(11)
    take_piece(12)
    for way in range(2):
        u_arrival(way, 3).wait_recv()

    total_rows = u_all.shape[0]
    index = lax.broadcasted_iota(jnp.int32, (1, total_rows), 1)
    by_group, by_adapter = up_rows.bit_length() - 1, up_rank.bit_length() - 1
    target = lax.shift_right_logical(index, by_group) * up_rank + (index & (up_rank - 1))
    holder = lax.shift_right_logical(index, by_adapter) & (adapters - 1)

    @pl.loop(0, segs)
    def _(s):
        yy = s // (2 * seg_block)
        line = lax.broadcasted_iota(jnp.int32, (double_rank, total_rows), 0)
        hit = (line == target + yy * rank) & (holder == adapter_of(group, s))
        pick = jnp.where(hit, 1.0, 0.0).astype(jnp.bfloat16)
        u_sel[s] = jnp.dot(pick, u_all[...], preferred_element_type=jnp.float32).astype(
            jnp.bfloat16
        )

    take_piece(13)
    hop2.wait_recv()
    low[core] = (kept[...] + swap_in[...].astype(jnp.float32)).astype(jnp.bfloat16)
    hop3 = remote(low.at[core], low.at[core], hop_send.at[2], hop_recv.at[2], (group, sibling))
    hop3.start()
    take_piece(pieces - 2)
    remote(
        low.at[1 - core], low.at[1 - core], hop_send.at[2], hop_recv.at[2], (group, sibling)
    ).wait_recv()

    @pl.loop(0, segs)
    def _(s):
        block, inner = s // seg_block, s % seg_block
        span_rows = pl.ds(pl.multiple_of(inner * seg_len, seg_len), seg_len)
        acc[block, span_rows, :] += jnp.dot(
            low[block % 2, span_rows, :], u_sel[s], preferred_element_type=jnp.float32
        )

    out[me] = acc[me].astype(jnp.bfloat16)
    out[sibling] = acc[sibling].astype(jnp.bfloat16)

    pair.wait_send()
    hop1.wait_send()
    hop2.wait_send()
    hop3.wait_send()
    for way in range(2):
        for k in range(4):
            one(way, k).wait_send()
            two(way, k).wait_send()
            three(way, k).wait_send()
        three_picked(way).wait_send()
        four_picked(way).wait_send()
        for step in range(4):
            u_copy(way, step).wait_send()

    @pl.loop(0, pieces - 2)
    def _(i):
        fwd_copy(i).wait_send()

    fwd_arrival(pieces - 2).wait_recv()
    add(diagonal, columns(pieces - 2, y))

    tail = range(pieces - 1, pieces - 1 + PARTS)
    final = pieces - 2 + PARTS
    start = near(n_dp - 1) * (4 * tile) + other_y * piece
    width = piece // PARTS
    early = pl.ds(pl.multiple_of(start, width), piece - width)
    for i in tail[:-1]:
        y_arrival(i).wait_recv()
        fwd_copy(i).start()
    add(across, early)
    for i in tail[:-1]:
        fwd_arrival(i).wait_recv()
    add(diagonal, early)
    y_arrival(final).wait_recv()
    fwd_copy(final).start()
    add(across, columns(final, y))
    out[across] = acc[across].astype(jnp.bfloat16)
    fwd_arrival(final).wait_recv()
    add(diagonal, columns(final, y))
    out[diagonal] = acc[diagonal].astype(jnp.bfloat16)
    for i in tail:
        y_copy(i).wait_send()
    for i in range(pieces - 2, pieces - 1 + PARTS):
        fwd_copy(i).wait_send()


def on_device(
    tokens,
    key_value_weight,
    adapter_down_weight,
    adapter_up_weight,
    adapter_per_request,
    request_per_segment,
):
    n_dp = lax.axis_size("dp")
    n_mp = lax.axis_size("mp")
    rows, depth = tokens.shape
    width = key_value_weight.shape[1]
    adapters, tile, double_rank = adapter_down_weight.shape
    up_rank = adapter_up_weight.shape[1]
    whole_tiles = tile % 256 == 0 and adapters % 4 == 0 and (adapters * up_rank) % 32 == 0
    powers = adapters & (adapters - 1) == 0 and up_rank & (up_rank - 1) == 0
    if n_mp != 4 or n_dp != 8 or not whole_tiles or not powers:
        return plain(
            tokens, key_value_weight, adapter_down_weight, adapter_up_weight,
            adapter_per_request, request_per_segment,
        )
    seg_group = request_per_segment.shape[0] // n_dp
    up_rows = adapters * up_rank
    bf16, f32 = jnp.bfloat16, jnp.float32
    dma = pltpu.SemaphoreType.DMA
    vmem = pl.BlockSpec(memory_space=pltpu.VMEM)
    result = pl.pallas_call(
        functools.partial(kernel, n_dp, up_rank),
        out_shape=jax.ShapeDtypeStruct((n_mp, rows, width), bf16),
        in_specs=[pl.BlockSpec(memory_space=pltpu.HBM)] * 6,
        out_specs=vmem,
        scratch_shapes=[
            pltpu.SMEM(adapter_per_request.shape, jnp.int32),
            pltpu.SMEM(request_per_segment.shape, jnp.int32),
            pltpu.VMEM((n_mp, rows, depth), bf16),
            pltpu.VMEM((depth, width), bf16),
            pltpu.VMEM((adapters, tile, double_rank), bf16),
            pltpu.VMEM((2, adapters, tile, double_rank), bf16),
            pltpu.VMEM((2, adapters, tile, double_rank), bf16),
            pltpu.VMEM((2, adapters, tile // 2, double_rank), bf16),
            pltpu.VMEM((2, seg_group, tile // 2, double_rank), bf16),
            pltpu.VMEM((2, seg_group, tile // 2, double_rank), bf16),
            pltpu.VMEM((2, seg_group, tile // 2, double_rank), bf16),
            pltpu.VMEM((2, seg_group, tile // 2, double_rank), bf16),
            pltpu.VMEM((n_dp * up_rows, width), bf16),
            pltpu.VMEM((n_mp, rows, width), f32),
            pltpu.VMEM((2, 2, rows, double_rank), f32),
            pltpu.VMEM((2, rows, double_rank), f32),
            pltpu.VMEM((rows, double_rank), f32),
            pltpu.VMEM((rows, double_rank), bf16),
            pltpu.VMEM((rows, double_rank), bf16),
            pltpu.VMEM((2, rows, double_rank), bf16),
            pltpu.VMEM((seg_group, double_rank, width), bf16),
            dma((6,)),
            dma,
            dma,
            dma((2 * n_dp + PARTS - 1,)),
            dma((2 * n_dp + PARTS - 1,)),
            dma((2 * n_dp + PARTS - 1,)),
            dma((2 * n_dp + PARTS - 1,)),
            dma((2, 14)),
            dma((2, 14)),
            dma((2, 4)),
            dma((2, 4)),
            dma((3,)),
            dma((3,)),
        ],
        compiler_params=pltpu.CompilerParams(
            collective_id=0, has_side_effects=True, vmem_limit_bytes=52 * 2**20
        ),
    )(
        *(
            pltpu.with_memory_space_constraint(a, pltpu.HBM)
            for a in (
                adapter_per_request, request_per_segment, tokens, key_value_weight,
                adapter_down_weight, adapter_up_weight.reshape(up_rows, width),
            )
        )
    )
    return result.reshape(n_mp * rows, width)


def solution(mesh):
    placed = (
        P(("dp", "mp"), None),
        P(None, "mp"),
        P(None, ("dp", "mp"), None),
        P(None, "dp", "mp"),
        P(),
        P(),
    )
    return jax.shard_map(
        on_device, mesh=mesh, in_specs=placed, out_specs=P("dp", "mp"), check_vma=False
    )
```

```python
import functools

import jax
import jax.numpy as jnp
from jax import lax
from jax.experimental import pallas as pl
from jax.experimental.pallas import tpu as pltpu
from jax.sharding import PartitionSpec as P

MESH = pl.DeviceIdType.MESH
AHEAD = 6
PARTS = 4


def plain(
    tokens,
    key_value_weight,
    adapter_down_weight,
    adapter_up_weight,
    adapter_per_request,
    request_per_segment,
):
    n_dp = lax.axis_size("dp")
    n_mp = lax.axis_size("mp")
    group = lax.axis_index("dp")
    column = lax.axis_index("mp")
    seg_total = request_per_segment.shape[0]
    seg_group = seg_total // n_dp
    seg_adapter = jnp.take(adapter_per_request, request_per_segment, axis=0)
    local_portion = lax.dynamic_slice_in_dim(seg_adapter, group * seg_group, seg_group)
    gathered = lax.all_gather(tokens, "mp", axis=0, tiled=True)
    rows = gathered.shape[0]
    seg_len = rows // seg_group
    width_tile = adapter_down_weight.shape[1]
    double_rank = adapter_down_weight.shape[2]
    rank = double_rank // 2
    column_tile = adapter_up_weight.shape[2]
    base = jnp.dot(gathered, key_value_weight, preferred_element_type=jnp.float32)
    strided = lax.dynamic_index_in_dim(
        gathered.reshape(rows, n_dp, n_mp, width_tile), column, 2, keepdims=False
    ).reshape(seg_group, seg_len, n_dp * width_tile)
    selected_factor = jnp.take(
        lax.all_gather(adapter_down_weight, "dp", axis=1, tiled=True), local_portion, axis=0
    )
    partial_low = jnp.einsum(
        "sti,sir->str", strided, selected_factor, preferred_element_type=jnp.float32
    )
    selected_factor = jnp.take(
        lax.all_gather(adapter_up_weight, "dp", axis=1, tiled=True), local_portion, axis=0
    )
    rank_output = lax.psum(partial_low, "mp").astype(jnp.bfloat16)
    key_width = n_mp * column_tile // 2
    half = column * column_tile // key_width
    low_half = lax.dynamic_slice_in_dim(rank_output, half * rank, rank, 2)
    delta = jnp.einsum(
        "str,src->stc", low_half, selected_factor, preferred_element_type=jnp.float32
    )
    return (base + delta.reshape(rows, column_tile)).astype(jnp.bfloat16)


def kernel(
    n_dp,
    up_rank,
    requests_in,
    segments_in,
    tok,
    weight,
    down,
    up,
    out,
    requests,
    segments,
    t_all,
    w_all,
    d_own,
    d_one,
    d_two,
    d_three,
    d_three_picked,
    d_four_picked,
    stage_three,
    stage_four,
    u_all,
    acc,
    part,
    part_in,
    swap_out,
    swap_in,
    low,
    u_sel,
    local_sem,
    pair_send,
    pair_recv,
    y_send,
    y_recv,
    fwd_send,
    fwd_recv,
    d_send,
    d_recv,
    u_send,
    u_recv,
    hop_send,
    hop_recv,
):
    group = lax.axis_index("dp")
    me = lax.axis_index("mp")
    y, core = me // 2, me % 2
    other_y = 1 - y
    sibling = y * 2 + (1 - core)
    across = other_y * 2 + core
    diagonal = other_y * 2 + (1 - core)

    rows, depth = tok.shape
    adapters, tile, double_rank = down.shape
    rank = double_rank // 2
    up_rows = up.shape[0]
    pieces = 2 * n_dp
    piece = 2 * tile
    span = n_dp // 2
    half_tile = tile // 2
    quarter = adapters // 4
    segs = segments.shape[0] // n_dp
    seg_block = segs // 4
    seg_len = rows // seg_block

    z, x = group // 2, group % 2
    place = z + x * (n_dp - 1 - 2 * z)

    def at_place(q):
        q = (q + 2 * n_dp) % n_dp
        side, step = q // span, q % span
        return (step + side * (span - 1 - 2 * step)) * 2 + side

    after, before = at_place(place + 1), at_place(place - 1)
    onward = (after, before)

    def adapter_of(g, seg):
        return requests[segments[g * segs + seg]]

    barrier = pltpu.get_barrier_semaphore()
    for partner in ((after, me), (before, me), (group, across), (group, sibling)):
        pl.semaphore_signal(barrier, inc=1, device_id=partner, device_id_type=MESH)
    pl.semaphore_wait(barrier, 4)

    def remote(src, dst, send, recv, partner):
        return pltpu.make_async_remote_copy(
            src_ref=src, dst_ref=dst, send_sem=send, recv_sem=recv,
            device_id=partner, device_id_type=MESH,
        )

    def quarter_of(k):
        return pl.ds(k * quarter, quarter)

    def one(way, k):
        return remote(
            down.at[quarter_of(k)], d_one.at[way, quarter_of(k)],
            d_send.at[way, k], d_recv.at[way, k], (onward[way], me),
        )

    def two(way, k):
        return remote(
            d_one.at[way, quarter_of(k)], d_two.at[way, quarter_of(k)],
            d_send.at[way, 4 + k], d_recv.at[way, 4 + k], (onward[way], me),
        )

    def three(way, k):
        return remote(
            d_two.at[way, quarter_of(k), pl.ds(way * half_tile, half_tile)],
            d_three.at[way, quarter_of(k)],
            d_send.at[way, 8 + k], d_recv.at[way, 8 + k], (onward[way], me),
        )

    def three_picked(way):
        return remote(
            stage_three.at[way], d_three_picked.at[way],
            d_send.at[way, 12], d_recv.at[way, 12], (onward[way], me),
        )

    def four_picked(way):
        return remote(
            stage_four.at[way], d_four_picked.at[way],
            d_send.at[way, 13], d_recv.at[way, 13], (onward[way], me),
        )

    def u_rows(way, step, block):
        if step < span - 1:
            return pl.ds(pl.multiple_of(block * up_rows, up_rows), up_rows)
        half = up_rows // 2
        return pl.ds(pl.multiple_of(block * up_rows + way * half, half), half)

    def u_copy(way, step):
        block = at_place(place - step) if way == 0 else at_place(place + step)
        there = u_rows(way, step, block)
        return remote(
            up if step == 0 else u_all.at[there], u_all.at[there],
            u_send.at[way, step], u_recv.at[way, step], (onward[way], me),
        )

    def u_arrival(way, step):
        block = at_place(place - 1 - step) if way == 0 else at_place(place + 1 + step)
        there = u_rows(way, step, block)
        return remote(
            u_all.at[there], u_all.at[there],
            u_send.at[way, step], u_recv.at[way, step], (onward[way], me),
        )

    def near(k):
        return at_place(place + (k + 1) // 2 * (1 - 2 * (k % 2)))

    def columns(i, side):
        part_of = i - (pieces - 1)
        if isinstance(i, int) and part_of >= 0:
            width = piece // PARTS
            start = near(n_dp - 1) * (4 * tile) + ((side + 1) % 2) * piece + part_of * width
            return pl.ds(pl.multiple_of(start, width), width)
        start = near(i % n_dp) * (4 * tile) + ((side + i // n_dp) % 2) * piece
        return pl.ds(pl.multiple_of(start, piece), piece)

    def y_copy(i):
        cols = columns(i, other_y)
        return remote(
            tok.at[:, cols], t_all.at[me, :, cols], y_send.at[i], y_recv.at[i], (group, across)
        )

    def y_arrival(i):
        cols = columns(i, y)
        return remote(
            tok.at[:, cols], t_all.at[across, :, cols], y_send.at[i], y_recv.at[i],
            (group, across),
        )

    def fwd_copy(i):
        cols = columns(i, y)
        return remote(
            t_all.at[across, :, cols], t_all.at[across, :, cols],
            fwd_send.at[i], fwd_recv.at[i], (group, sibling),
        )

    def fwd_arrival(i):
        cols = columns(i, y)
        return remote(
            t_all.at[diagonal, :, cols], t_all.at[diagonal, :, cols],
            fwd_send.at[i], fwd_recv.at[i], (group, sibling),
        )

    for i in range(AHEAD):
        y_copy(i).start()
    for k in range(4):
        for way in range(2):
            one(way, k).start()
    t_local = pltpu.make_async_copy(tok, t_all.at[me], local_sem.at[0])
    w_local = pltpu.make_async_copy(weight, w_all, local_sem.at[1])
    d_local = pltpu.make_async_copy(down, d_own, local_sem.at[2])
    u_local = pltpu.make_async_copy(
        up, u_all.at[pl.ds(pl.multiple_of(group * up_rows, up_rows), up_rows)], local_sem.at[3]
    )
    r_local = pltpu.make_async_copy(requests_in, requests, local_sem.at[4])
    s_local = pltpu.make_async_copy(segments_in, segments, local_sem.at[5])
    r_local.start()
    s_local.start()
    t_local.start()
    w_local.start()
    d_local.start()
    u_local.start()
    pair = remote(tok, t_all.at[me], pair_send, pair_recv, (group, sibling))
    pair.start()

    acc[...] = jnp.zeros_like(acc)
    part[...] = jnp.zeros_like(part)

    def add(block, cols):
        acc[block] += jnp.dot(
            t_all[block, :, cols], w_all[cols, :], preferred_element_type=jnp.float32
        )

    def add_whole(block):
        @pl.loop(0, n_dp)
        def _(k):
            add(block, pl.ds(pl.multiple_of(k * 4 * tile, 4 * tile), 4 * tile))

    def take_piece(i):
        y_arrival(i).wait_recv()
        fwd_copy(i).start()
        y_copy(i).wait_send()

        @pl.when(i + AHEAD < pieces - 2)
        def _():
            y_copy(i + AHEAD).start()

        add(across, columns(i, y))

        @pl.when(i > 0)
        def _():
            fwd_arrival(i - 1).wait_recv()
            add(diagonal, columns(i - 1, y))

    def add_low(blocks, factors):
        @pl.loop(0, segs)
        def _(s):
            block, inner = s // seg_block, s % seg_block
            span_rows = pl.ds(pl.multiple_of(inner * seg_len, seg_len), seg_len)
            adapter = adapter_of(group, s)
            total = part[block % 2, block // 2, span_rows, :]
            for g, factor in zip(blocks, factors):
                cols = pl.ds(pl.multiple_of(g * 4 * tile + me * tile, tile), tile)
                total += jnp.dot(
                    t_all[block, span_rows, cols], factor(adapter, s),
                    preferred_element_type=jnp.float32,
                )
            part[block % 2, block // 2, span_rows, :] = total

    t_local.wait()
    w_local.wait()
    add_whole(me)

    @pl.loop(0, 4)
    def _(k):
        for way in range(2):
            one(way, k).wait_recv()
            two(way, k).start()

        @pl.when(k == 1)
        def _():
            remote(tok, t_all.at[sibling], pair_send, pair_recv, (group, sibling)).wait_recv()
            add_whole(sibling)

        @pl.when(k > 0)
        def _():
            take_piece(k - 1)

    d_local.wait()
    u_local.wait()
    r_local.wait()
    s_local.wait()

    @pl.loop(0, 4)
    def _(k):
        for way in range(2):
            two(way, k).wait_recv()
            three(way, k).start()
        take_piece(k + 3)

        @pl.when(k == 1)
        def _():
            add_low(
                [group, before, after],
                [lambda a, s: d_own[a], lambda a, s: d_one[0, a], lambda a, s: d_one[1, a]],
            )

    @pl.loop(0, segs)
    def _(s):
        for way in range(2):
            stage_three[way, s] = d_two[
                way, adapter_of(onward[way], s), pl.ds((1 - way) * half_tile, half_tile), :
            ]

    for way in range(2):
        three_picked(way).start()
    add_low(
        [at_place(place - 2), at_place(place + 2)],
        [lambda a, s: d_two[0, a], lambda a, s: d_two[1, a]],
    )

    @pl.loop(0, 2)
    def _(h):
        take_piece(h + 7)
        for j in range(2):
            for way in range(2):
                three(way, 2 * h + j).wait_recv()

    @pl.loop(0, segs)
    def _(s):
        for way in range(2):
            stage_four[way, s] = d_three[way, adapter_of(onward[way], s)]

    for way in range(2):
        four_picked(way).start()
    for way in range(2):
        u_copy(way, 0).start()
    take_piece(9)
    for way in range(2):
        three_picked(way).wait_recv()
    add_low(
        [at_place(place - 3), at_place(place + 3)],
        [
            lambda a, s: jnp.concatenate([d_three[0, a], d_three_picked[0, s]], axis=0),
            lambda a, s: jnp.concatenate([d_three_picked[1, s], d_three[1, a]], axis=0),
        ],
    )
    take_piece(10)
    for way in range(2):
        four_picked(way).wait_recv()
    add_low(
        [at_place(place + 4)],
        [lambda a, s: jnp.concatenate([d_four_picked[0, s], d_four_picked[1, s]], axis=0)],
    )

    hop1 = remote(part.at[1 - core], part_in, hop_send.at[0], hop_recv.at[0], (group, sibling))
    hop1.start()
    hop1.wait_recv()
    q0 = part[core, 0] + part_in[0]
    q1 = part[core, 1] + part_in[1]
    key_part = jnp.concatenate([q0[:, :rank], q1[:, :rank]], axis=1)
    value_part = jnp.concatenate([q0[:, rank:], q1[:, rank:]], axis=1)
    swap_out[0] = jnp.where(y == 0, value_part, key_part)
    swap_out[1] = jnp.where(y == 0, key_part, value_part)
    hop2 = remote(swap_out.at[0], swap_in, hop_send.at[1], hop_recv.at[1], (group, across))
    hop2.start()
    for i in range(pieces - 2, pieces - 1 + PARTS):
        y_copy(i).start()
    for way in range(2):
        u_arrival(way, 0).wait_recv()
        u_copy(way, 1).start()

    take_piece(11)
    for way in range(2):
        u_arrival(way, 1).wait_recv()
        u_copy(way, 2).start()
    take_piece(12)
    for way in range(2):
        u_arrival(way, 2).wait_recv()
        u_copy(way, 3).start()
    take_piece(13)
    hop2.wait_recv()
    low[core] = (swap_out[1] + swap_in[...]).astype(jnp.bfloat16)
    hop3 = remote(low.at[core], low.at[core], hop_send.at[2], hop_recv.at[2], (group, sibling))
    hop3.start()
    for way in range(2):
        u_arrival(way, 3).wait_recv()

    total_rows = u_all.shape[0]
    index = lax.broadcasted_iota(jnp.int32, (1, total_rows), 1)
    by_group, by_adapter = up_rows.bit_length() - 1, up_rank.bit_length() - 1
    target = lax.shift_right_logical(index, by_group) * up_rank + (index & (up_rank - 1))
    holder = lax.shift_right_logical(index, by_adapter) & (adapters - 1)

    @pl.loop(0, segs)
    def _(s):
        yy = s // (2 * seg_block)
        line = lax.broadcasted_iota(jnp.int32, (double_rank, total_rows), 0)
        hit = (line == target + yy * rank) & (holder == adapter_of(group, s))
        pick = jnp.where(hit, 1.0, 0.0).astype(jnp.bfloat16)
        u_sel[s] = jnp.dot(pick, u_all[...], preferred_element_type=jnp.float32).astype(
            jnp.bfloat16
        )

    remote(
        low.at[1 - core], low.at[1 - core], hop_send.at[2], hop_recv.at[2], (group, sibling)
    ).wait_recv()

    @pl.loop(0, segs)
    def _(s):
        block, inner = s // seg_block, s % seg_block
        span_rows = pl.ds(pl.multiple_of(inner * seg_len, seg_len), seg_len)
        acc[block, span_rows, :] += jnp.dot(
            low[block % 2, span_rows, :], u_sel[s], preferred_element_type=jnp.float32
        )

    out[me] = acc[me].astype(jnp.bfloat16)
    out[sibling] = acc[sibling].astype(jnp.bfloat16)

    take_piece(pieces - 2)
    pair.wait_send()
    hop1.wait_send()
    hop2.wait_send()
    hop3.wait_send()
    for way in range(2):
        for k in range(4):
            one(way, k).wait_send()
            two(way, k).wait_send()
            three(way, k).wait_send()
        three_picked(way).wait_send()
        four_picked(way).wait_send()
        for step in range(4):
            u_copy(way, step).wait_send()

    @pl.loop(0, pieces - 2)
    def _(i):
        fwd_copy(i).wait_send()

    fwd_arrival(pieces - 2).wait_recv()
    add(diagonal, columns(pieces - 2, y))

    tail = range(pieces - 1, pieces - 1 + PARTS)
    final = pieces - 2 + PARTS
    start = near(n_dp - 1) * (4 * tile) + other_y * piece
    width = piece // PARTS
    early = pl.ds(pl.multiple_of(start, width), piece - width)
    for i in tail[:-1]:
        y_arrival(i).wait_recv()
        fwd_copy(i).start()
    add(across, early)
    for i in tail[:-1]:
        fwd_arrival(i).wait_recv()
    add(diagonal, early)
    y_arrival(final).wait_recv()
    fwd_copy(final).start()
    add(across, columns(final, y))
    out[across] = acc[across].astype(jnp.bfloat16)
    fwd_arrival(final).wait_recv()
    add(diagonal, columns(final, y))
    out[diagonal] = acc[diagonal].astype(jnp.bfloat16)
    for i in tail:
        y_copy(i).wait_send()
    for i in range(pieces - 2, pieces - 1 + PARTS):
        fwd_copy(i).wait_send()


def on_device(
    tokens,
    key_value_weight,
    adapter_down_weight,
    adapter_up_weight,
    adapter_per_request,
    request_per_segment,
):
    n_dp = lax.axis_size("dp")
    n_mp = lax.axis_size("mp")
    rows, depth = tokens.shape
    width = key_value_weight.shape[1]
    adapters, tile, double_rank = adapter_down_weight.shape
    up_rank = adapter_up_weight.shape[1]
    whole_tiles = tile % 256 == 0 and adapters % 4 == 0 and (adapters * up_rank) % 32 == 0
    powers = adapters & (adapters - 1) == 0 and up_rank & (up_rank - 1) == 0
    if n_mp != 4 or n_dp != 8 or not whole_tiles or not powers:
        return plain(
            tokens, key_value_weight, adapter_down_weight, adapter_up_weight,
            adapter_per_request, request_per_segment,
        )
    seg_group = request_per_segment.shape[0] // n_dp
    up_rows = adapters * up_rank
    bf16, f32 = jnp.bfloat16, jnp.float32
    dma = pltpu.SemaphoreType.DMA
    vmem = pl.BlockSpec(memory_space=pltpu.VMEM)
    result = pl.pallas_call(
        functools.partial(kernel, n_dp, up_rank),
        out_shape=jax.ShapeDtypeStruct((n_mp, rows, width), bf16),
        in_specs=[pl.BlockSpec(memory_space=pltpu.HBM)] * 6,
        out_specs=vmem,
        scratch_shapes=[
            pltpu.SMEM(adapter_per_request.shape, jnp.int32),
            pltpu.SMEM(request_per_segment.shape, jnp.int32),
            pltpu.VMEM((n_mp, rows, depth), bf16),
            pltpu.VMEM((depth, width), bf16),
            pltpu.VMEM((adapters, tile, double_rank), bf16),
            pltpu.VMEM((2, adapters, tile, double_rank), bf16),
            pltpu.VMEM((2, adapters, tile, double_rank), bf16),
            pltpu.VMEM((2, adapters, tile // 2, double_rank), bf16),
            pltpu.VMEM((2, seg_group, tile // 2, double_rank), bf16),
            pltpu.VMEM((2, seg_group, tile // 2, double_rank), bf16),
            pltpu.VMEM((2, seg_group, tile // 2, double_rank), bf16),
            pltpu.VMEM((2, seg_group, tile // 2, double_rank), bf16),
            pltpu.VMEM((n_dp * up_rows, width), bf16),
            pltpu.VMEM((n_mp, rows, width), f32),
            pltpu.VMEM((2, 2, rows, double_rank), f32),
            pltpu.VMEM((2, rows, double_rank), f32),
            pltpu.VMEM((2, rows, double_rank), f32),
            pltpu.VMEM((rows, double_rank), f32),
            pltpu.VMEM((2, rows, double_rank), bf16),
            pltpu.VMEM((seg_group, double_rank, width), bf16),
            dma((6,)),
            dma,
            dma,
            dma((2 * n_dp + PARTS - 1,)),
            dma((2 * n_dp + PARTS - 1,)),
            dma((2 * n_dp + PARTS - 1,)),
            dma((2 * n_dp + PARTS - 1,)),
            dma((2, 14)),
            dma((2, 14)),
            dma((2, 4)),
            dma((2, 4)),
            dma((3,)),
            dma((3,)),
        ],
        compiler_params=pltpu.CompilerParams(
            collective_id=0, has_side_effects=True, vmem_limit_bytes=52 * 2**20
        ),
    )(
        *(
            pltpu.with_memory_space_constraint(a, pltpu.HBM)
            for a in (
                adapter_per_request, request_per_segment, tokens, key_value_weight,
                adapter_down_weight, adapter_up_weight.reshape(up_rows, width),
            )
        )
    )
    return result.reshape(n_mp * rows, width)


def solution(mesh):
    placed = (
        P(("dp", "mp"), None),
        P(None, "mp"),
        P(None, ("dp", "mp"), None),
        P(None, "dp", "mp"),
        P(),
        P(),
    )
    return jax.shard_map(
        on_device, mesh=mesh, in_specs=placed, out_specs=P("dp", "mp"), check_vma=False
    )
```

```python
import functools

import jax
import jax.numpy as jnp
from jax import lax
from jax.experimental import pallas as pl
from jax.experimental.pallas import tpu as pltpu
from jax.sharding import PartitionSpec as P

MESH = pl.DeviceIdType.MESH
AHEAD = 6
PARTS = 4


def plain(
    tokens,
    key_value_weight,
    adapter_down_weight,
    adapter_up_weight,
    adapter_per_request,
    request_per_segment,
):
    n_dp = lax.axis_size("dp")
    n_mp = lax.axis_size("mp")
    group = lax.axis_index("dp")
    column = lax.axis_index("mp")
    seg_total = request_per_segment.shape[0]
    seg_group = seg_total // n_dp
    seg_adapter = jnp.take(adapter_per_request, request_per_segment, axis=0)
    local_portion = lax.dynamic_slice_in_dim(seg_adapter, group * seg_group, seg_group)
    gathered = lax.all_gather(tokens, "mp", axis=0, tiled=True)
    rows = gathered.shape[0]
    seg_len = rows // seg_group
    width_tile = adapter_down_weight.shape[1]
    double_rank = adapter_down_weight.shape[2]
    rank = double_rank // 2
    column_tile = adapter_up_weight.shape[2]
    base = jnp.dot(gathered, key_value_weight, preferred_element_type=jnp.float32)
    strided = lax.dynamic_index_in_dim(
        gathered.reshape(rows, n_dp, n_mp, width_tile), column, 2, keepdims=False
    ).reshape(seg_group, seg_len, n_dp * width_tile)
    selected_factor = jnp.take(
        lax.all_gather(adapter_down_weight, "dp", axis=1, tiled=True), local_portion, axis=0
    )
    partial_low = jnp.einsum(
        "sti,sir->str", strided, selected_factor, preferred_element_type=jnp.float32
    )
    selected_factor = jnp.take(
        lax.all_gather(adapter_up_weight, "dp", axis=1, tiled=True), local_portion, axis=0
    )
    rank_output = lax.psum(partial_low, "mp").astype(jnp.bfloat16)
    key_width = n_mp * column_tile // 2
    half = column * column_tile // key_width
    low_half = lax.dynamic_slice_in_dim(rank_output, half * rank, rank, 2)
    delta = jnp.einsum(
        "str,src->stc", low_half, selected_factor, preferred_element_type=jnp.float32
    )
    return (base + delta.reshape(rows, column_tile)).astype(jnp.bfloat16)


def kernel(
    n_dp,
    up_rank,
    requests_in,
    segments_in,
    tok,
    weight,
    down,
    up,
    out,
    requests,
    segments,
    t_all,
    w_all,
    d_own,
    d_one,
    d_two,
    d_three,
    d_three_picked,
    d_four_picked,
    stage_three,
    stage_four,
    u_all,
    acc,
    part,
    part_in,
    swap_out,
    swap_in,
    low,
    u_sel,
    local_sem,
    pair_send,
    pair_recv,
    y_send,
    y_recv,
    fwd_send,
    fwd_recv,
    d_send,
    d_recv,
    u_send,
    u_recv,
    hop_send,
    hop_recv,
):
    group = lax.axis_index("dp")
    me = lax.axis_index("mp")
    y, core = me // 2, me % 2
    other_y = 1 - y
    sibling = y * 2 + (1 - core)
    across = other_y * 2 + core
    diagonal = other_y * 2 + (1 - core)

    rows, depth = tok.shape
    adapters, tile, double_rank = down.shape
    rank = double_rank // 2
    up_rows = up.shape[0]
    pieces = 2 * n_dp
    piece = 2 * tile
    span = n_dp // 2
    half_tile = tile // 2
    quarter = adapters // 4
    segs = segments.shape[0] // n_dp
    seg_block = segs // 4
    seg_len = rows // seg_block

    z, x = group // 2, group % 2
    place = z + x * (n_dp - 1 - 2 * z)

    def at_place(q):
        q = (q + 2 * n_dp) % n_dp
        side, step = q // span, q % span
        return (step + side * (span - 1 - 2 * step)) * 2 + side

    after, before = at_place(place + 1), at_place(place - 1)
    onward = (after, before)

    def adapter_of(g, seg):
        return requests[segments[g * segs + seg]]

    barrier = pltpu.get_barrier_semaphore()
    for partner in ((after, me), (before, me), (group, across), (group, sibling)):
        pl.semaphore_signal(barrier, inc=1, device_id=partner, device_id_type=MESH)
    pl.semaphore_wait(barrier, 4)

    def remote(src, dst, send, recv, partner):
        return pltpu.make_async_remote_copy(
            src_ref=src, dst_ref=dst, send_sem=send, recv_sem=recv,
            device_id=partner, device_id_type=MESH,
        )

    def quarter_of(k):
        return pl.ds(k * quarter, quarter)

    def one(way, k):
        return remote(
            down.at[quarter_of(k)], d_one.at[way, quarter_of(k)],
            d_send.at[way, k], d_recv.at[way, k], (onward[way], me),
        )

    def two(way, k):
        return remote(
            d_one.at[way, quarter_of(k)], d_two.at[way, quarter_of(k)],
            d_send.at[way, 4 + k], d_recv.at[way, 4 + k], (onward[way], me),
        )

    def three(way, k):
        return remote(
            d_two.at[way, quarter_of(k), pl.ds(way * half_tile, half_tile)],
            d_three.at[way, quarter_of(k)],
            d_send.at[way, 8 + k], d_recv.at[way, 8 + k], (onward[way], me),
        )

    def three_picked(way):
        return remote(
            stage_three.at[way], d_three_picked.at[way],
            d_send.at[way, 12], d_recv.at[way, 12], (onward[way], me),
        )

    def four_picked(way):
        return remote(
            stage_four.at[way], d_four_picked.at[way],
            d_send.at[way, 13], d_recv.at[way, 13], (onward[way], me),
        )

    def u_rows(way, step, block):
        if step < span - 1:
            return pl.ds(pl.multiple_of(block * up_rows, up_rows), up_rows)
        half = up_rows // 2
        return pl.ds(pl.multiple_of(block * up_rows + way * half, half), half)

    def u_copy(way, step):
        block = at_place(place - step) if way == 0 else at_place(place + step)
        there = u_rows(way, step, block)
        return remote(
            up if step == 0 else u_all.at[there], u_all.at[there],
            u_send.at[way, step], u_recv.at[way, step], (onward[way], me),
        )

    def u_arrival(way, step):
        block = at_place(place - 1 - step) if way == 0 else at_place(place + 1 + step)
        there = u_rows(way, step, block)
        return remote(
            u_all.at[there], u_all.at[there],
            u_send.at[way, step], u_recv.at[way, step], (onward[way], me),
        )

    def near(k):
        return at_place(place + (k + 1) // 2 * (1 - 2 * (k % 2)))

    def columns(i, side):
        part_of = i - (pieces - 1)
        if isinstance(i, int) and part_of >= 0:
            width = piece // PARTS
            start = near(n_dp - 1) * (4 * tile) + ((side + 1) % 2) * piece + part_of * width
            return pl.ds(pl.multiple_of(start, width), width)
        start = near(i % n_dp) * (4 * tile) + ((side + i // n_dp) % 2) * piece
        return pl.ds(pl.multiple_of(start, piece), piece)

    def y_copy(i):
        cols = columns(i, other_y)
        return remote(
            tok.at[:, cols], t_all.at[me, :, cols], y_send.at[i], y_recv.at[i], (group, across)
        )

    def y_arrival(i):
        cols = columns(i, y)
        return remote(
            tok.at[:, cols], t_all.at[across, :, cols], y_send.at[i], y_recv.at[i],
            (group, across),
        )

    def fwd_copy(i):
        cols = columns(i, y)
        return remote(
            t_all.at[across, :, cols], t_all.at[across, :, cols],
            fwd_send.at[i], fwd_recv.at[i], (group, sibling),
        )

    def fwd_arrival(i):
        cols = columns(i, y)
        return remote(
            t_all.at[diagonal, :, cols], t_all.at[diagonal, :, cols],
            fwd_send.at[i], fwd_recv.at[i], (group, sibling),
        )

    for i in range(AHEAD):
        y_copy(i).start()
    for k in range(4):
        for way in range(2):
            one(way, k).start()
    t_local = pltpu.make_async_copy(tok, t_all.at[me], local_sem.at[0])
    w_local = pltpu.make_async_copy(weight, w_all, local_sem.at[1])
    d_local = pltpu.make_async_copy(down, d_own, local_sem.at[2])
    u_local = pltpu.make_async_copy(
        up, u_all.at[pl.ds(pl.multiple_of(group * up_rows, up_rows), up_rows)], local_sem.at[3]
    )
    r_local = pltpu.make_async_copy(requests_in, requests, local_sem.at[4])
    s_local = pltpu.make_async_copy(segments_in, segments, local_sem.at[5])
    r_local.start()
    s_local.start()
    t_local.start()
    w_local.start()
    d_local.start()
    u_local.start()
    pair = remote(tok, t_all.at[me], pair_send, pair_recv, (group, sibling))
    pair.start()

    acc[...] = jnp.zeros_like(acc)
    part[...] = jnp.zeros_like(part)

    def add(block, cols):
        acc[block] += jnp.dot(
            t_all[block, :, cols], w_all[cols, :], preferred_element_type=jnp.float32
        )

    def add_whole(block):
        @pl.loop(0, n_dp)
        def _(k):
            add(block, pl.ds(pl.multiple_of(k * 4 * tile, 4 * tile), 4 * tile))

    def take_piece(i):
        y_arrival(i).wait_recv()
        fwd_copy(i).start()
        y_copy(i).wait_send()

        @pl.when(i + AHEAD < pieces - 1)
        def _():
            y_copy(i + AHEAD).start()

        add(across, columns(i, y))

        @pl.when(i > 0)
        def _():
            fwd_arrival(i - 1).wait_recv()
            add(diagonal, columns(i - 1, y))

    def add_low(blocks, factors):
        @pl.loop(0, segs)
        def _(s):
            block, inner = s // seg_block, s % seg_block
            span_rows = pl.ds(pl.multiple_of(inner * seg_len, seg_len), seg_len)
            adapter = adapter_of(group, s)
            total = part[block % 2, block // 2, span_rows, :]
            for g, factor in zip(blocks, factors):
                cols = pl.ds(pl.multiple_of(g * 4 * tile + me * tile, tile), tile)
                total += jnp.dot(
                    t_all[block, span_rows, cols], factor(adapter, s),
                    preferred_element_type=jnp.float32,
                )
            part[block % 2, block // 2, span_rows, :] = total

    t_local.wait()
    w_local.wait()
    add_whole(me)

    @pl.loop(0, 4)
    def _(k):
        for way in range(2):
            one(way, k).wait_recv()
            two(way, k).start()

        @pl.when(k == 1)
        def _():
            remote(tok, t_all.at[sibling], pair_send, pair_recv, (group, sibling)).wait_recv()
            add_whole(sibling)

        @pl.when(k > 0)
        def _():
            take_piece(k - 1)

    d_local.wait()
    u_local.wait()
    r_local.wait()
    s_local.wait()

    @pl.loop(0, 4)
    def _(k):
        for way in range(2):
            two(way, k).wait_recv()
            three(way, k).start()
        take_piece(k + 3)

        @pl.when(k == 1)
        def _():
            add_low(
                [group, before, after],
                [lambda a, s: d_own[a], lambda a, s: d_one[0, a], lambda a, s: d_one[1, a]],
            )

    @pl.loop(0, segs)
    def _(s):
        for way in range(2):
            stage_three[way, s] = d_two[
                way, adapter_of(onward[way], s), pl.ds((1 - way) * half_tile, half_tile), :
            ]

    for way in range(2):
        three_picked(way).start()
    add_low(
        [at_place(place - 2), at_place(place + 2)],
        [lambda a, s: d_two[0, a], lambda a, s: d_two[1, a]],
    )

    @pl.loop(0, 2)
    def _(h):
        take_piece(h + 7)
        for j in range(2):
            for way in range(2):
                three(way, 2 * h + j).wait_recv()

    @pl.loop(0, segs)
    def _(s):
        for way in range(2):
            stage_four[way, s] = d_three[way, adapter_of(onward[way], s)]

    for way in range(2):
        four_picked(way).start()
    for way in range(2):
        u_copy(way, 0).start()
    take_piece(9)
    for way in range(2):
        three_picked(way).wait_recv()
    add_low(
        [at_place(place - 3), at_place(place + 3)],
        [
            lambda a, s: jnp.concatenate([d_three[0, a], d_three_picked[0, s]], axis=0),
            lambda a, s: jnp.concatenate([d_three_picked[1, s], d_three[1, a]], axis=0),
        ],
    )
    take_piece(10)
    for way in range(2):
        four_picked(way).wait_recv()
    add_low(
        [at_place(place + 4)],
        [lambda a, s: jnp.concatenate([d_four_picked[0, s], d_four_picked[1, s]], axis=0)],
    )

    hop1 = remote(part.at[1 - core], part_in, hop_send.at[0], hop_recv.at[0], (group, sibling))
    hop1.start()
    hop1.wait_recv()
    q0 = part[core, 0] + part_in[0]
    q1 = part[core, 1] + part_in[1]
    key_part = jnp.concatenate([q0[:, :rank], q1[:, :rank]], axis=1)
    value_part = jnp.concatenate([q0[:, rank:], q1[:, rank:]], axis=1)
    swap_out[0] = jnp.where(y == 0, value_part, key_part)
    swap_out[1] = jnp.where(y == 0, key_part, value_part)
    hop2 = remote(swap_out.at[0], swap_in, hop_send.at[1], hop_recv.at[1], (group, across))
    hop2.start()
    for i in range(pieces - 1, pieces - 1 + PARTS):
        y_copy(i).start()
    for way in range(2):
        u_arrival(way, 0).wait_recv()
        u_copy(way, 1).start()

    take_piece(11)
    for way in range(2):
        u_arrival(way, 1).wait_recv()
        u_copy(way, 2).start()
    take_piece(12)
    for way in range(2):
        u_arrival(way, 2).wait_recv()
        u_copy(way, 3).start()
    take_piece(13)
    for way in range(2):
        u_arrival(way, 3).wait_recv()

    total_rows = u_all.shape[0]
    index = lax.broadcasted_iota(jnp.int32, (1, total_rows), 1)
    by_group, by_adapter = up_rows.bit_length() - 1, up_rank.bit_length() - 1
    target = lax.shift_right_logical(index, by_group) * up_rank + (index & (up_rank - 1))
    holder = lax.shift_right_logical(index, by_adapter) & (adapters - 1)

    @pl.loop(0, segs)
    def _(s):
        yy = s // (2 * seg_block)
        line = lax.broadcasted_iota(jnp.int32, (double_rank, total_rows), 0)
        hit = (line == target + yy * rank) & (holder == adapter_of(group, s))
        pick = jnp.where(hit, 1.0, 0.0).astype(jnp.bfloat16)
        u_sel[s] = jnp.dot(pick, u_all[...], preferred_element_type=jnp.float32).astype(
            jnp.bfloat16
        )

    hop2.wait_recv()
    low[core] = (swap_out[1] + swap_in[...]).astype(jnp.bfloat16)
    hop3 = remote(low.at[core], low.at[core], hop_send.at[2], hop_recv.at[2], (group, sibling))
    hop3.start()
    take_piece(pieces - 2)
    remote(
        low.at[1 - core], low.at[1 - core], hop_send.at[2], hop_recv.at[2], (group, sibling)
    ).wait_recv()

    @pl.loop(0, segs)
    def _(s):
        block, inner = s // seg_block, s % seg_block
        span_rows = pl.ds(pl.multiple_of(inner * seg_len, seg_len), seg_len)
        acc[block, span_rows, :] += jnp.dot(
            low[block % 2, span_rows, :], u_sel[s], preferred_element_type=jnp.float32
        )

    out[me] = acc[me].astype(jnp.bfloat16)
    out[sibling] = acc[sibling].astype(jnp.bfloat16)

    pair.wait_send()
    hop1.wait_send()
    hop2.wait_send()
    hop3.wait_send()
    for way in range(2):
        for k in range(4):
            one(way, k).wait_send()
            two(way, k).wait_send()
            three(way, k).wait_send()
        three_picked(way).wait_send()
        four_picked(way).wait_send()
        for step in range(4):
            u_copy(way, step).wait_send()

    @pl.loop(0, pieces - 2)
    def _(i):
        fwd_copy(i).wait_send()

    fwd_arrival(pieces - 2).wait_recv()
    add(diagonal, columns(pieces - 2, y))

    tail = range(pieces - 1, pieces - 1 + PARTS)
    final = pieces - 2 + PARTS
    start = near(n_dp - 1) * (4 * tile) + other_y * piece
    width = piece // PARTS
    early = pl.ds(pl.multiple_of(start, width), piece - width)
    for i in tail[:-1]:
        y_arrival(i).wait_recv()
        fwd_copy(i).start()
    add(across, early)
    for i in tail[:-1]:
        fwd_arrival(i).wait_recv()
    add(diagonal, early)
    y_arrival(final).wait_recv()
    fwd_copy(final).start()
    add(across, columns(final, y))
    out[across] = acc[across].astype(jnp.bfloat16)
    fwd_arrival(final).wait_recv()
    add(diagonal, columns(final, y))
    out[diagonal] = acc[diagonal].astype(jnp.bfloat16)
    for i in tail:
        y_copy(i).wait_send()
    for i in range(pieces - 2, pieces - 1 + PARTS):
        fwd_copy(i).wait_send()


def on_device(
    tokens,
    key_value_weight,
    adapter_down_weight,
    adapter_up_weight,
    adapter_per_request,
    request_per_segment,
):
    n_dp = lax.axis_size("dp")
    n_mp = lax.axis_size("mp")
    rows, depth = tokens.shape
    width = key_value_weight.shape[1]
    adapters, tile, double_rank = adapter_down_weight.shape
    up_rank = adapter_up_weight.shape[1]
    whole_tiles = tile % 256 == 0 and adapters % 4 == 0 and (adapters * up_rank) % 32 == 0
    powers = adapters & (adapters - 1) == 0 and up_rank & (up_rank - 1) == 0
    if n_mp != 4 or n_dp != 8 or not whole_tiles or not powers:
        return plain(
            tokens, key_value_weight, adapter_down_weight, adapter_up_weight,
            adapter_per_request, request_per_segment,
        )
    seg_group = request_per_segment.shape[0] // n_dp
    up_rows = adapters * up_rank
    bf16, f32 = jnp.bfloat16, jnp.float32
    dma = pltpu.SemaphoreType.DMA
    vmem = pl.BlockSpec(memory_space=pltpu.VMEM)
    result = pl.pallas_call(
        functools.partial(kernel, n_dp, up_rank),
        out_shape=jax.ShapeDtypeStruct((n_mp, rows, width), bf16),
        in_specs=[pl.BlockSpec(memory_space=pltpu.HBM)] * 6,
        out_specs=vmem,
        scratch_shapes=[
            pltpu.SMEM(adapter_per_request.shape, jnp.int32),
            pltpu.SMEM(request_per_segment.shape, jnp.int32),
            pltpu.VMEM((n_mp, rows, depth), bf16),
            pltpu.VMEM((depth, width), bf16),
            pltpu.VMEM((adapters, tile, double_rank), bf16),
            pltpu.VMEM((2, adapters, tile, double_rank), bf16),
            pltpu.VMEM((2, adapters, tile, double_rank), bf16),
            pltpu.VMEM((2, adapters, tile // 2, double_rank), bf16),
            pltpu.VMEM((2, seg_group, tile // 2, double_rank), bf16),
            pltpu.VMEM((2, seg_group, tile // 2, double_rank), bf16),
            pltpu.VMEM((2, seg_group, tile // 2, double_rank), bf16),
            pltpu.VMEM((2, seg_group, tile // 2, double_rank), bf16),
            pltpu.VMEM((n_dp * up_rows, width), bf16),
            pltpu.VMEM((n_mp, rows, width), f32),
            pltpu.VMEM((2, 2, rows, double_rank), f32),
            pltpu.VMEM((2, rows, double_rank), f32),
            pltpu.VMEM((2, rows, double_rank), f32),
            pltpu.VMEM((rows, double_rank), f32),
            pltpu.VMEM((2, rows, double_rank), bf16),
            pltpu.VMEM((seg_group, double_rank, width), bf16),
            dma((6,)),
            dma,
            dma,
            dma((2 * n_dp + PARTS - 1,)),
            dma((2 * n_dp + PARTS - 1,)),
            dma((2 * n_dp + PARTS - 1,)),
            dma((2 * n_dp + PARTS - 1,)),
            dma((2, 14)),
            dma((2, 14)),
            dma((2, 4)),
            dma((2, 4)),
            dma((3,)),
            dma((3,)),
        ],
        compiler_params=pltpu.CompilerParams(
            collective_id=0, has_side_effects=True, vmem_limit_bytes=52 * 2**20
        ),
    )(
        *(
            pltpu.with_memory_space_constraint(a, pltpu.HBM)
            for a in (
                adapter_per_request, request_per_segment, tokens, key_value_weight,
                adapter_down_weight, adapter_up_weight.reshape(up_rows, width),
            )
        )
    )
    return result.reshape(n_mp * rows, width)


def solution(mesh):
    placed = (
        P(("dp", "mp"), None),
        P(None, "mp"),
        P(None, ("dp", "mp"), None),
        P(None, "dp", "mp"),
        P(),
        P(),
    )
    return jax.shard_map(
        on_device, mesh=mesh, in_specs=placed, out_specs=P("dp", "mp"), check_vma=False
    )
```
